256 devices in a mesh: tm: 8 (over x, z_lo), space: 32 (over z_hi, y, core).
Axes of the slice: x: 4, y: 4, z: 8 (z_hi: 4, z_lo: 2; z = z_hi * 2 + z_lo), core: 2. Of those that a mesh axis runs over, the one named last changes fastest.
Arguments:
- snapshots: float32 [2048, 2, 131072], P('tm', None, 'space'), may hold values from -120 to 120
- quad_weights: float32 [131072], P('space'), may hold values from 0.25 to 4
Outputs:
- mode_blocks: float32 [8, 64, 2, 131072], P(None, 'tm', None, 'space')
- upper_factor: float32 [64, 2, 8, 8], P('tm')
The draws below stay inside these ranges and needn't reach their ends.
All inputs are finite; a program needn't handle non-finite values.
Results may differ from the reference program's by a relative error of at most 0.00013.
Values sent between devices are 32-bit elements; how exact they have to be, the bound alone decides.
A program may use at most 128 MiB of HBM per device.

```python
import math
import jax
import jax.numpy as jnp
from jax import lax

NB = 8
NFFT = 256
KF = 64
SNAPS = 2048
PTS = 131072


def draw_snapshots(key, part):
    key_noise = jax.random.fold_in(key, 11)
    key_rough = jax.random.fold_in(key, 23)
    time_pos = jnp.arange(SNAPS, dtype=jnp.float32) / (SNAPS - 1) - 0.5
    point_pos = jnp.arange(PTS, dtype=jnp.float32) / (PTS - 1) - 0.5
    roughness = jnp.exp(jax.random.uniform(key_rough, (PTS,), jnp.float32, math.log(0.3), math.log(3.0)))
    noise_draw = jnp.clip(jax.random.normal(key_noise, (SNAPS, 2, PTS), jnp.float32), -6.0, 6.0)
    time_ramp = jnp.exp(math.log(10.0) * time_pos)
    point_trend = jnp.exp(math.log(3.0) * point_pos)
    values = noise_draw * time_ramp[:, None, None] * (roughness * point_trend)[None, None, :]
    return values.astype(jnp.float32)


def level_of(own_key, extent, shards, least, largest):
    def one(position, blocks):
        draws = jax.random.uniform(jax.random.fold_in(jax.random.fold_in(own_key, 6), position), (blocks,), jnp.float32, least / len(shards), largest / len(shards))
        return jnp.repeat(jnp.exp(draws), extent[position] // blocks).reshape((-1,) + (1,) * (len(extent) - position - 1))

    level = one(*shards[0])
    for cut in shards[1:]:
        level = level * one(*cut)
    return level


def setup_inputs(seed: int = 0) -> dict:
    key_list = jax.random.split(jax.random.key(seed), 3)
    snapshots = draw_snapshots(jax.random.fold_in(key_list[2], 71), 0)
    quad_weights = jnp.clip(jnp.exp(math.log(4.0) - 2.7725887 * jax.random.uniform(key_list[1], (PTS,), jnp.float32) ** level_of(key_list[1], (PTS,), ((0, 32),), -0.2, 0.2)), 0.25, 4.0)
    return {"snapshots": snapshots, "quad_weights": quad_weights}


def dft_tables():
    column = jnp.arange(NFFT, dtype=jnp.int32)
    freqs = jnp.arange(KF, dtype=jnp.int32)
    window = 0.54 - 0.46 * jnp.cos(2.0 * math.pi * column.astype(jnp.float32) / NFFT)
    phase = (freqs[:, None] * column[None, :] % NFFT).astype(jnp.float32)
    angles = 2.0 * math.pi * phase / NFFT
    return (window[None, :] * jnp.cos(angles), window[None, :] * jnp.sin(angles))

def transform(centered, cos_tab, sin_tab):
    highest = lax.Precision.HIGHEST
    spec_re = jnp.einsum('kj,bjp->bkp', cos_tab, centered[:, :, 0], precision=highest) + jnp.einsum('kj,bjp->bkp', sin_tab, centered[:, :, 1], precision=highest)
    spec_im = jnp.einsum('kj,bjp->bkp', cos_tab, centered[:, :, 1], precision=highest) - jnp.einsum('kj,bjp->bkp', sin_tab, centered[:, :, 0], precision=highest)
    return jnp.stack([spec_re, spec_im], axis=2)

def local_gram(spectra, scaled):
    highest = lax.Precision.HIGHEST
    weighted = spectra * scaled
    gram_re = jnp.einsum('afp,bfp->abf', weighted[:, :, 0], spectra[:, :, 0], precision=highest) + jnp.einsum('afp,bfp->abf', weighted[:, :, 1], spectra[:, :, 1], precision=highest)
    gram_im = jnp.einsum('afp,bfp->abf', weighted[:, :, 0], spectra[:, :, 1], precision=highest) - jnp.einsum('afp,bfp->abf', weighted[:, :, 1], spectra[:, :, 0], precision=highest)
    return (gram_re, gram_im)

def stack_rows(table):
    return jnp.stack([jnp.stack(entries, 0) for entries in table], 0)

def cholesky_upper(gram_re, gram_im):
    size_n = gram_re.shape[0]
    zero_row = jnp.zeros_like(gram_re[0, 0])
    upper_re = [[zero_row] * size_n for row_i in range(size_n)]
    upper_im = [[zero_row] * size_n for row_i in range(size_n)]
    for j in range(size_n):
        pivot_sq = gram_re[j, j]
        for k in range(j):
            pivot_sq = pivot_sq - upper_re[k][j] * upper_re[k][j] - upper_im[k][j] * upper_im[k][j]
        pivot_root = jnp.sqrt(pivot_sq)
        upper_re[j][j] = pivot_root
        for i in range(j + 1, size_n):
            acc_re = gram_re[j, i]
            acc_im = gram_im[j, i]
            for k in range(j):
                acc_re = acc_re - (upper_re[k][j] * upper_re[k][i] + upper_im[k][j] * upper_im[k][i])
                acc_im = acc_im - (upper_re[k][j] * upper_im[k][i] - upper_im[k][j] * upper_re[k][i])
            upper_re[j][i] = acc_re / pivot_root
            upper_im[j][i] = acc_im / pivot_root
    return (stack_rows(upper_re), stack_rows(upper_im))

def invert_upper(upper_re, upper_im):
    size_n = upper_re.shape[0]
    zero_row = jnp.zeros_like(upper_re[0, 0])
    inv_re = [[zero_row] * size_n for row_i in range(size_n)]
    inv_im = [[zero_row] * size_n for row_i in range(size_n)]
    for j in range(size_n):
        inv_re[j][j] = 1.0 / upper_re[j, j]
        for i in range(j - 1, -1, -1):
            acc_re = zero_row
            acc_im = zero_row
            for k in range(i + 1, j + 1):
                acc_re = acc_re + upper_re[i, k] * inv_re[k][j] - upper_im[i, k] * inv_im[k][j]
                acc_im = acc_im + upper_re[i, k] * inv_im[k][j] + upper_im[i, k] * inv_re[k][j]
            inv_re[i][j] = -acc_re / upper_re[i, i]
            inv_im[i][j] = -acc_im / upper_re[i, i]
    return (stack_rows(inv_re), stack_rows(inv_im))

def apply_inverse(spectra, inv_re, inv_im):
    highest = lax.Precision.HIGHEST
    mode_re = jnp.einsum('afp,abf->bfp', spectra[:, :, 0], inv_re, precision=highest) - jnp.einsum('afp,abf->bfp', spectra[:, :, 1], inv_im, precision=highest)
    mode_im = jnp.einsum('afp,abf->bfp', spectra[:, :, 0], inv_im, precision=highest) + jnp.einsum('afp,abf->bfp', spectra[:, :, 1], inv_re, precision=highest)
    return jnp.stack([mode_re, mode_im], axis=2)

def reference(snapshots, quad_weights):
    time_mean = lax.optimization_barrier(jnp.sum(snapshots, axis=0)) / (NB * NFFT)
    centered = (snapshots - time_mean).reshape(NB, NFFT, 2, PTS)
    cos_tab, sin_tab = dft_tables()
    spectra = transform(centered, cos_tab, sin_tab)
    gram_re, gram_im = local_gram(spectra, quad_weights / PTS)
    fac_re, fac_im = cholesky_upper(gram_re, gram_im)
    inv_re, inv_im = invert_upper(fac_re, fac_im)
    mode_blocks = apply_inverse(spectra, inv_re, inv_im)
    upper_factor = jnp.transpose(jnp.stack([fac_re, fac_im], 0), (3, 0, 1, 2))
    return (mode_blocks, upper_factor)
```

```python
import math

import jax
import jax.numpy as jnp
from jax import lax
from jax.sharding import PartitionSpec as P

NB = 8
NFFT = 256
KF = 64


def dft_tables():
    column = jnp.arange(NFFT, dtype=jnp.int32)
    freqs = jnp.arange(KF, dtype=jnp.int32)
    window = 0.54 - 0.46 * jnp.cos(2.0 * math.pi * column.astype(jnp.float32) / NFFT)
    phase = (freqs[:, None] * column[None, :] % NFFT).astype(jnp.float32)
    angles = 2.0 * math.pi * phase / NFFT
    return (window[None, :] * jnp.cos(angles), window[None, :] * jnp.sin(angles))


def transform(centered, cos_tab, sin_tab):
    highest = lax.Precision.HIGH
    spec_re = jnp.einsum("kj,bjp->bkp", cos_tab, centered[:, :, 0], precision=highest) + jnp.einsum(
        "kj,bjp->bkp", sin_tab, centered[:, :, 1], precision=highest
    )
    spec_im = jnp.einsum("kj,bjp->bkp", cos_tab, centered[:, :, 1], precision=highest) - jnp.einsum(
        "kj,bjp->bkp", sin_tab, centered[:, :, 0], precision=highest
    )
    return jnp.stack([spec_re, spec_im], axis=2)


def local_gram(spectra, scaled):
    highest = lax.Precision.HIGH
    weighted = spectra * scaled
    gram_re = jnp.einsum(
        "afp,bfp->abf", weighted[:, :, 0], spectra[:, :, 0], precision=highest
    ) + jnp.einsum("afp,bfp->abf", weighted[:, :, 1], spectra[:, :, 1], precision=highest)
    gram_im = jnp.einsum(
        "afp,bfp->abf", weighted[:, :, 0], spectra[:, :, 1], precision=highest
    ) - jnp.einsum("afp,bfp->abf", weighted[:, :, 1], spectra[:, :, 0], precision=highest)
    return (gram_re, gram_im)


def stack_rows(table):
    return jnp.stack([jnp.stack(entries, 0) for entries in table], 0)


def cholesky_upper(gram_re, gram_im):
    size_n = gram_re.shape[0]
    zero_row = jnp.zeros_like(gram_re[0, 0])
    upper_re = [[zero_row] * size_n for row_i in range(size_n)]
    upper_im = [[zero_row] * size_n for row_i in range(size_n)]
    for j in range(size_n):
        pivot_sq = gram_re[j, j]
        for k in range(j):
            pivot_sq = pivot_sq - upper_re[k][j] * upper_re[k][j] - upper_im[k][j] * upper_im[k][j]
        pivot_root = jnp.sqrt(pivot_sq)
        upper_re[j][j] = pivot_root
        for i in range(j + 1, size_n):
            acc_re = gram_re[j, i]
            acc_im = gram_im[j, i]
            for k in range(j):
                acc_re = acc_re - (
                    upper_re[k][j] * upper_re[k][i] + upper_im[k][j] * upper_im[k][i]
                )
                acc_im = acc_im - (
                    upper_re[k][j] * upper_im[k][i] - upper_im[k][j] * upper_re[k][i]
                )
            upper_re[j][i] = acc_re / pivot_root
            upper_im[j][i] = acc_im / pivot_root
    return (stack_rows(upper_re), stack_rows(upper_im))


def invert_upper(upper_re, upper_im):
    size_n = upper_re.shape[0]
    zero_row = jnp.zeros_like(upper_re[0, 0])
    inv_re = [[zero_row] * size_n for row_i in range(size_n)]
    inv_im = [[zero_row] * size_n for row_i in range(size_n)]
    for j in range(size_n):
        inv_re[j][j] = 1.0 / upper_re[j, j]
        for i in range(j - 1, -1, -1):
            acc_re = zero_row
            acc_im = zero_row
            for k in range(i + 1, j + 1):
                acc_re = acc_re + upper_re[i, k] * inv_re[k][j] - upper_im[i, k] * inv_im[k][j]
                acc_im = acc_im + upper_re[i, k] * inv_im[k][j] + upper_im[i, k] * inv_re[k][j]
            inv_re[i][j] = -acc_re / upper_re[i, i]
            inv_im[i][j] = -acc_im / upper_re[i, i]
    return (stack_rows(inv_re), stack_rows(inv_im))


def apply_inverse(spectra, inv_re, inv_im):
    highest = lax.Precision.HIGH
    mode_re = jnp.einsum("afp,abf->bfp", spectra[:, :, 0], inv_re, precision=highest) - jnp.einsum(
        "afp,abf->bfp", spectra[:, :, 1], inv_im, precision=highest
    )
    mode_im = jnp.einsum("afp,abf->bfp", spectra[:, :, 0], inv_im, precision=highest) + jnp.einsum(
        "afp,abf->bfp", spectra[:, :, 1], inv_re, precision=highest
    )
    return jnp.stack([mode_re, mode_im], axis=2)


def body(snapshots, quad_weights):
    cell_count = snapshots.shape[2]
    blocks_dev = snapshots.shape[0] // NFFT
    point_total = cell_count * lax.axis_size("space")
    block_total = jnp.sum(snapshots, axis=0)
    time_mean = lax.psum(block_total, "tm") / (NB * NFFT)
    centered = snapshots.reshape(blocks_dev, NFFT, 2, cell_count) - time_mean
    cos_tab, sin_tab = dft_tables()
    spectra = transform(centered, cos_tab, sin_tab)
    scaled = quad_weights / point_total
    owned_spec = lax.all_to_all(spectra, "tm", split_axis=1, concat_axis=0, tiled=True)
    share = jnp.stack(local_gram(owned_spec, scaled), 0)
    gram_re, gram_im = lax.psum(share, "space")
    fac_re, fac_im = cholesky_upper(gram_re, gram_im)
    inv_re, inv_im = invert_upper(fac_re, fac_im)
    mode_blocks = apply_inverse(owned_spec, inv_re, inv_im)
    upper_factor = jnp.transpose(jnp.stack([fac_re, fac_im], 0), (3, 0, 1, 2))
    return (mode_blocks, upper_factor)


def solution(mesh):
    placed = (P("tm", None, "space"), P("space"))
    return jax.shard_map(
        body,
        mesh=mesh,
        in_specs=placed,
        out_specs=(P(None, "tm", None, "space"), P("tm", None, None, None)),
        check_vma=False,
    )
```

```python
import functools
import math

import jax
import jax.numpy as jnp
import ml_dtypes
import numpy as np
from jax import lax
from jax.experimental import pallas as pl
from jax.experimental.pallas import tpu as pltpu
from jax.sharding import PartitionSpec as P

NB = 8
NFFT = 256
KF = 64
LANES = 128
EARLY = 2
SPLIT = 6
MESH = pl.DeviceIdType.MESH

PAIRS_RE = [(a, b) for a in range(NB) for b in range(a, NB)]
PAIRS_IM = [(a, b) for a in range(NB) for b in range(a + 1, NB)]
SLOT_RE = {pair: i for i, pair in enumerate(PAIRS_RE)}
SLOT_IM = {pair: len(PAIRS_RE) + i for i, pair in enumerate(PAIRS_IM)}
SLOTS = len(PAIRS_RE) + len(PAIRS_IM)


def tables():
    j = np.arange(NFFT)
    k = np.arange(KF)
    window = 0.54 - 0.46 * np.cos(2.0 * math.pi * j / NFFT)
    angles = 2.0 * math.pi * (k[:, None] * j[None, :] % NFFT) / NFFT
    cos_tab = window * np.cos(angles)
    sin_tab = window * np.sin(angles)
    full = np.zeros((2, KF, NFFT, 2))
    full[0, :, :, 0] = cos_tab
    full[0, :, :, 1] = sin_tab
    full[1, :, :, 0] = -sin_tab
    full[1, :, :, 1] = cos_tab
    full = full.reshape(2 * KF, 2 * NFFT).astype(np.float32)
    high = full.astype(ml_dtypes.bfloat16)
    low = (full - high.astype(np.float32)).astype(ml_dtypes.bfloat16)
    ones = np.ones((1, LANES))
    window_re = (cos_tab.sum(1)[:, None] * ones).astype(np.float32)
    window_im = (-sin_tab.sum(1)[:, None] * ones).astype(np.float32)
    return np.concatenate([high, low], 0), np.stack([window_re, window_im], 0)


def turned(z, even):
    return jnp.where(even, pltpu.roll(z, 7, 0), -pltpu.roll(z, 1, 0))


def cholesky(gram_re, gram_im):
    up_re, up_im, diag_inv = {}, {}, {}
    for j in range(NB):
        pivot = gram_re[j, j]
        for k in range(j):
            pivot = pivot - (up_re[k, j] * up_re[k, j] + up_im[k, j] * up_im[k, j])
        inv = lax.rsqrt(pivot)
        inv = inv * (1.5 - 0.5 * ((pivot * inv) * inv))
        diag_inv[j] = inv
        up_re[j, j] = pivot * inv
        for i in range(j + 1, NB):
            acc_re, acc_im = gram_re[j, i], gram_im[j, i]
            for k in range(j):
                acc_re = acc_re - (up_re[k, j] * up_re[k, i] + up_im[k, j] * up_im[k, i])
                acc_im = acc_im - (up_re[k, j] * up_im[k, i] - up_im[k, j] * up_re[k, i])
            up_re[j, i] = acc_re * inv
            up_im[j, i] = acc_im * inv
    inv_re, inv_im = {}, {}
    for j in range(NB):
        inv_re[j, j] = diag_inv[j]
        for i in range(j - 1, -1, -1):
            acc_re = up_re[i, j] * inv_re[j, j]
            acc_im = up_im[i, j] * inv_re[j, j]
            for k in range(i + 1, j):
                acc_re = acc_re + up_re[i, k] * inv_re[k, j] - up_im[i, k] * inv_im[k, j]
                acc_im = acc_im + up_re[i, k] * inv_im[k, j] + up_im[i, k] * inv_re[k, j]
            inv_re[i, j] = -acc_re * diag_inv[i]
            inv_im[i, j] = -acc_im * diag_inv[i]
    return up_re, up_im, inv_re, inv_im


def kernel(
    point_total, x_hbm, w_hbm, tab_hbm, win_hbm, modes_hbm, factor_ref,
    xs, tab, win, wgt, wgt2, spec, sums, sums_in, mean_part, mean, recv, turn, prod, acc, inverse, modes,
    share, core_in, half, space_in,
    x_sem, in_sem, send_sem, recv_sem, sums_sem, mean_sem, small_sem, core_sem, space_sem, out_sem,
):
    tm = lax.axis_index("tm")
    sp = lax.axis_index("space")
    points = xs.shape[0]
    rows = 2 * points
    steps = points // 4
    per = KF // NB

    z_hi, y, core = lax.div(sp, 8), lax.rem(lax.div(sp, 2), 4), lax.rem(sp, 2)
    mates = [lax.rem(tm + d, NB) for d in range(1, NB)]
    core_peer = z_hi * 8 + y * 2 + (1 - core)
    space_peers = [
        lax.rem(z_hi + dz, 4) * 8 + lax.rem(y + dy, 4) * 2 + core
        for dz in range(4)
        for dy in range(4)
        if (dz, dy) != (0, 0)
    ]

    def x_copy(pt):
        return pltpu.make_async_copy(x_hbm.at[:, pt], xs.at[pt], x_sem.at[pt // 4])

    tab_copy = pltpu.make_async_copy(tab_hbm, tab, in_sem.at[0])
    win_copy = pltpu.make_async_copy(win_hbm, win, in_sem.at[1])
    wgt_copy = pltpu.make_async_copy(w_hbm, wgt, in_sem.at[2])
    for pt in range(4):
        x_copy(pt).start()
    tab_copy.start()
    win_copy.start()
    for pt in range(4, points):
        x_copy(pt).start()
    wgt_copy.start()

    barrier = pltpu.get_barrier_semaphore()
    for mate in mates:
        pl.semaphore_signal(barrier, 1, device_id=(mate, sp), device_id_type=MESH)
    for peer in [core_peer, *space_peers]:
        pl.semaphore_signal(barrier, 1, device_id=(tm, peer), device_id_type=MESH)

    row8 = lax.broadcasted_iota(jnp.int32, (8, LANES), 0)
    lane8 = lax.broadcasted_iota(jnp.int32, (8, LANES), 1)
    even = lax.rem(row8, 2) == 0
    spec_rows = spec.reshape(KF * rows, LANES)

    def remote(src, dst, recv_at, mate=None, peer=None, sent=None):
        return pltpu.make_async_remote_copy(
            src, dst, send_sem if sent is None else sent, recv_at,
            device_id=(tm if mate is None else mate, sp if peer is None else peer), device_id_type=MESH,
        )

    def transform_step(q):
        pltpu.make_async_copy(xs.at[pl.ds(4 * q, 4)], xs.at[pl.ds(4 * q, 4)], x_sem.at[q]).wait()
        highs, lows, bases = [], [], []
        totals = None
        for i in range(4):
            v = xs.at[4 * q + i].reshape(2 * NFFT, LANES)[...]
            base = v[0:8]
            base = base + pltpu.roll(base, 4, 0)
            base = (base + pltpu.roll(base, 2, 0)) * 0.25
            d = v.reshape(NFFT // 4, 8, LANES) - base[None]
            total = jnp.sum(d, axis=0)
            total = total + pltpu.roll(total, 4, 0)
            total = total + pltpu.roll(total, 2, 0) + base * NFFT
            totals = total if i == 0 else jnp.where(lax.div(row8, 2) == i, total, totals)
            d = d.reshape(2 * NFFT, LANES)
            high = d.astype(jnp.bfloat16)
            highs.append(high)
            lows.append((d - high.astype(jnp.float32)).astype(jnp.bfloat16))
            bases.append(base)
        both = jnp.dot(tab[...], jnp.concatenate(highs, 1), preferred_element_type=jnp.float32)
        rest = jnp.dot(tab[: 2 * KF], jnp.concatenate(lows, 1), preferred_element_type=jnp.float32)
        out = both[: 2 * KF] + both[2 * KF :] + rest
        for i in range(4):
            at = slice(i * LANES, (i + 1) * LANES)
            base_re, base_im = bases[i][0:1], bases[i][1:2]
            spec_rows[pl.ds(8 * q + 2 * i, KF, stride=rows), :] = (
                out[:KF, at] + (win[0] * base_re - win[1] * base_im)
            )
            spec_rows[pl.ds(8 * q + 2 * i + 1, KF, stride=rows), :] = (
                out[KF:, at] + (win[0] * base_im + win[1] * base_re)
            )
        sums[pl.ds(pl.multiple_of(8 * q, 8), 8), :] = totals

    def early_sends(q):
        at = pl.ds(pl.multiple_of(8 * q, 8), 8)
        for mate in mates:
            remote(
                spec.at[mate, pl.ds(0, EARLY), at], recv.at[pl.ds(0, EARLY), tm, at], recv_sem.at[0], mate=mate
            ).start()

    tab_copy.wait()
    win_copy.wait()
    transform_step(0)
    pl.semaphore_wait(barrier, len(mates) + 1 + len(space_peers))
    early_sends(0)

    @pl.loop(1, steps)
    def _(q):
        transform_step(q)
        early_sends(q)

    pltpu.make_async_copy(spec.at[tm, pl.ds(0, EARLY)], recv.at[pl.ds(0, EARLY), tm], recv_sem.at[0]).start()
    for mate in mates:
        remote(
            sums.at[pl.ds(pl.multiple_of(8 * mate, 8), 8)], sums_in.at[tm], sums_sem, mate=mate, sent=small_sem.at[0]
        ).start()
    pltpu.make_async_copy(sums.at[pl.ds(pl.multiple_of(8 * tm, 8), 8)], sums_in.at[tm], sums_sem).start()
    for f in range(EARLY, per):
        for mate in mates:
            remote(spec.at[mate, f], recv.at[f, tm], recv_sem.at[f], mate=mate).start()
        pltpu.make_async_copy(spec.at[tm, f], recv.at[f, tm], recv_sem.at[f]).start()

    pltpu.make_async_copy(sums_in, sums_in, sums_sem).wait()
    part = sums_in[0]
    for a in range(1, NB):
        part = part + sums_in[a]
    mean_part[...] = part * (1.0 / (NB * NFFT))
    for mate in mates:
        remote(mean_part, mean.at[tm], mean_sem, mate=mate, sent=small_sem.at[1]).start()
    pltpu.make_async_copy(mean_part, mean.at[tm], mean_sem).start()
    wgt_copy.wait()
    scaled = wgt[...] / point_total
    wgt2[pl.ds(0, points, stride=2), :] = scaled
    wgt2[pl.ds(1, points, stride=2), :] = scaled
    pltpu.make_async_copy(mean, mean, mean_sem).wait()

    groups = rows // 8

    def gram_step(f, total):
        win_re = jnp.broadcast_to(win[0, pl.ds(per * tm + f, 1), :], (8, LANES))
        win_im = jnp.broadcast_to(win[1, pl.ds(per * tm + f, 1), :], (8, LANES))
        for g in range(groups):
            at = pl.ds(8 * g, 8)
            m = mean[g]
            shift = win_re * m - win_im * turned(m, even)
            weight = wgt2[at, :]
            for a in range(NB):
                z = recv[f, a, at, :] - shift
                recv[f, a, at, :] = z
                turn[f, a, at, :] = turned(z, even)
                prod[a, at, :] = z * weight
        for a in range(NB):
            sums_re = {}
            sums_im = {}
            for g in range(groups):
                at = pl.ds(8 * g, 8)
                p = prod[a, at, :]
                for b in range(a, NB):
                    term = p * recv[f, b, at, :]
                    sums_re[b] = term if g == 0 else sums_re[b] + term
                    if b > a:
                        term = p * turn[f, b, at, :]
                        sums_im[b] = term if g == 0 else sums_im[b] + term
            for b in range(a, NB):
                acc[pl.ds(8 * SLOT_RE[a, b], 8), :] = sums_re[b]
                if b > a:
                    acc[pl.ds(8 * SLOT_IM[a, b], 8), :] = sums_im[b]
        folded = acc[pl.ds(0, SLOTS, stride=8), :]
        for s in range(1, 8):
            folded = folded + acc[pl.ds(s, SLOTS, stride=8), :]
        folded = jnp.concatenate([folded, jnp.zeros((LANES - SLOTS, LANES), jnp.float32)], 0)
        line = lax.dot_general(
            jnp.ones((8, LANES), jnp.float32), folded, (((1,), (1,)), ((), ())),
            precision=lax.Precision.HIGHEST, preferred_element_type=jnp.float32,
        )
        return jnp.where(row8 == f, line, total)

    def waited_gram_step(f, total):
        pltpu.make_async_copy(recv.at[f], recv.at[f], recv_sem.at[f]).wait()
        return gram_step(f, total)

    def core_start(n, total):
        share[n] = total
        remote(share.at[n], core_in.at[n], core_sem.at[n, 0], peer=core_peer, sent=core_sem.at[n, 1]).start()

    def space_start(n):
        pltpu.make_async_copy(core_in.at[n], core_in.at[n], core_sem.at[n, 0]).wait()
        half[n] = share[n] + core_in[n]
        for i, peer in enumerate(space_peers):
            remote(half.at[n], space_in.at[n, i], space_sem.at[n, 0], peer=peer, sent=space_sem.at[n, 1]).start()

    def factored(n, factor):
        pltpu.make_async_copy(space_in.at[n], space_in.at[n], space_sem.at[n, 0]).wait()
        terms = [half[n]] + [space_in[n, i] for i in range(len(space_peers))]
        while len(terms) > 1:
            terms = [a + b for a, b in zip(terms[::2], terms[1::2])]
        gram = terms[0]
        spread = [jnp.broadcast_to(gram[:, i : i + 1], (8, LANES)) for i in range(SLOTS)]
        gram_re = {pair: spread[SLOT_RE[pair]] for pair in PAIRS_RE}
        gram_im = {pair: spread[SLOT_IM[pair]] for pair in PAIRS_IM}
        zero = jnp.zeros((8, LANES), jnp.float32)
        up_re, up_im, inv_re, inv_im = cholesky(
            gram_re, {**gram_im, **{(j, j): zero for j in range(NB)}}
        )
        for pair in PAIRS_RE:
            inverse[SLOT_RE[pair]] = inv_re[pair]
        for pair in PAIRS_IM:
            inverse[SLOT_IM[pair]] = inv_im[pair]
        lines = zero
        for a, b in PAIRS_RE:
            lines = jnp.where(lane8 == (NB - 1 - a) * NB + b, up_re[a, b], lines)
        for a, b in PAIRS_IM:
            lines = jnp.where(lane8 == NB * NB + (NB - 1 - a) * NB + b, up_im[a, b], lines)
        return lines if factor is None else jnp.where(row8 >= SPLIT, lines, factor)

    def apply_step(f):
        co_re = {p: jnp.broadcast_to(inverse[SLOT_RE[p], pl.ds(f, 1), :], (8, LANES)) for p in PAIRS_RE}
        co_im = {p: jnp.broadcast_to(inverse[SLOT_IM[p], pl.ds(f, 1), :], (8, LANES)) for p in PAIRS_IM}
        for b in range(NB):
            for g in range(groups):
                at = pl.ds(8 * g, 8)
                total = recv[f, 0, at, :] * co_re[0, b]
                for a in range(1, b + 1):
                    total = total + recv[f, a, at, :] * co_re[a, b]
                for a in range(b):
                    total = total - turn[f, a, at, :] * co_im[a, b]
                modes[b, f, at, :] = total
        pltpu.make_async_copy(modes.at[:, f], modes_hbm.at[:, f], out_sem).start()

    pltpu.make_async_copy(recv.at[pl.ds(0, EARLY)], recv.at[pl.ds(0, EARLY)], recv_sem.at[0]).wait()
    none = jnp.zeros((8, LANES), jnp.float32)
    first = lax.fori_loop(0, EARLY, gram_step, none)
    first = lax.fori_loop(EARLY, SPLIT, waited_gram_step, first)
    core_start(0, first)
    second = waited_gram_step(SPLIT, none)
    space_start(0)
    second = lax.fori_loop(SPLIT + 1, per, waited_gram_step, second)
    core_start(1, second)
    space_start(1)
    factor = factored(0, None)
    pl.loop(0, SPLIT)(apply_step)
    factor = factored(1, factor)
    pl.loop(SPLIT, per)(apply_step)
    for f in range(per):
        line = jnp.broadcast_to(factor[f : f + 1], (8, LANES))
        for c in range(2):
            upper_half = line if c == 1 else pltpu.roll(line, LANES // 2, 1)
            factor_ref[f, c] = pltpu.roll(upper_half, NB, 1, stride=NB, stride_axis=0)[:, :NB]

    sent = spec.at[pl.ds(0, NB - 1)]
    pltpu.make_async_copy(sent, sent, send_sem).wait()
    sent = sums_in.at[pl.ds(0, NB - 1)]
    for i in range(2):
        pltpu.make_async_copy(sent, sent, small_sem.at[i]).wait()
        pltpu.make_async_copy(core_in.at[i], core_in.at[i], core_sem.at[i, 1]).wait()
        pltpu.make_async_copy(space_in.at[i], space_in.at[i], space_sem.at[i, 1]).wait()
    pltpu.make_async_copy(modes, modes_hbm, out_sem).wait()


def body(snapshots, quad_weights):
    cell_count = snapshots.shape[2]
    points = cell_count // LANES
    rows = 2 * points
    per = KF // NB
    point_total = cell_count * lax.axis_size("space")
    others = lax.axis_size("space") // 2 - 1
    x = snapshots.reshape(NFFT, 2, points, LANES).transpose(0, 2, 1, 3)
    tab, win = tables()
    f32 = jnp.float32
    anywhere = pl.BlockSpec(memory_space=pl.ANY)
    dma = pltpu.SemaphoreType.DMA
    modes, factor = pl.pallas_call(
        functools.partial(kernel, point_total),
        out_shape=(
            jax.ShapeDtypeStruct((NB, per, rows, LANES), f32),
            jax.ShapeDtypeStruct((per, 2, NB, NB), f32),
        ),
        in_specs=[anywhere] * 4,
        out_specs=(anywhere, pl.BlockSpec(memory_space=pltpu.VMEM)),
        scratch_shapes=[
            pltpu.VMEM((points, NFFT, 2, LANES), f32),
            pltpu.VMEM((4 * KF, 2 * NFFT), jnp.bfloat16),
            pltpu.VMEM((2, KF, LANES), f32),
            pltpu.VMEM((points, LANES), f32),
            pltpu.VMEM((rows, LANES), f32),
            pltpu.VMEM((NB, per, rows, LANES), f32),
            pltpu.VMEM((rows, LANES), f32),
            pltpu.VMEM((NB, 8, LANES), f32),
            pltpu.VMEM((8, LANES), f32),
            pltpu.VMEM((NB, 8, LANES), f32),
            pltpu.VMEM((per, NB, rows, LANES), f32),
            pltpu.VMEM((per, NB, rows, LANES), f32),
            pltpu.VMEM((NB, rows, LANES), f32),
            pltpu.VMEM((SLOTS * 8, LANES), f32),
            pltpu.VMEM((SLOTS, 8, LANES), f32),
            pltpu.VMEM((NB, per, rows, LANES), f32),
            pltpu.VMEM((2, 8, LANES), f32),
            pltpu.VMEM((2, 8, LANES), f32),
            pltpu.VMEM((2, 8, LANES), f32),
            pltpu.VMEM((2, others, 8, LANES), f32),
            dma((points // 4,)),
            dma((3,)),
            dma,
            dma((per,)),
            dma,
            dma,
            dma((2,)),
            dma((2, 2)),
            dma((2, 2)),
            dma,
        ],
        compiler_params=pltpu.CompilerParams(
            collective_id=0, has_side_effects=True, vmem_limit_bytes=48 * 2**20
        ),
    )(x, quad_weights.reshape(points, LANES), jnp.asarray(tab), jnp.asarray(win))
    modes = modes.reshape(NB, per, points, 2, LANES).transpose(0, 1, 3, 2, 4)
    return (modes.reshape(NB, per, 2, cell_count), factor)


def solution(mesh):
    placed = (P("tm", None, "space"), P("space"))
    return jax.shard_map(
        body,
        mesh=mesh,
        in_specs=placed,
        out_specs=(P(None, "tm", None, "space"), P("tm", None, None, None)),
        check_vma=False,
    )
```

```python
import functools
import math

import jax
import jax.numpy as jnp
import ml_dtypes
import numpy as np
from jax import lax
from jax.experimental import pallas as pl
from jax.experimental.pallas import tpu as pltpu
from jax.sharding import PartitionSpec as P

NB = 8
NFFT = 256
KF = 64
LANES = 128
EARLY = 2
SPLIT = 6
FILL = 3
WINDOW = 8
MESH = pl.DeviceIdType.MESH

PAIRS_RE = [(a, b) for a in range(NB) for b in range(a, NB)]
PAIRS_IM = [(a, b) for a in range(NB) for b in range(a + 1, NB)]
SLOT_RE = {pair: i for i, pair in enumerate(PAIRS_RE)}
SLOT_IM = {pair: len(PAIRS_RE) + i for i, pair in enumerate(PAIRS_IM)}
SLOTS = len(PAIRS_RE) + len(PAIRS_IM)


def tables():
    j = np.arange(NFFT)
    k = np.arange(KF)
    window = 0.54 - 0.46 * np.cos(2.0 * math.pi * j / NFFT)
    angles = 2.0 * math.pi * (k[:, None] * j[None, :] % NFFT) / NFFT
    cos_tab = window * np.cos(angles)
    sin_tab = window * np.sin(angles)
    full = np.zeros((2, KF, NFFT, 2))
    full[0, :, :, 0] = cos_tab
    full[0, :, :, 1] = sin_tab
    full[1, :, :, 0] = -sin_tab
    full[1, :, :, 1] = cos_tab
    full = full.reshape(2 * KF, 2 * NFFT).astype(np.float32)
    high = full.astype(ml_dtypes.bfloat16)
    low = (full - high.astype(np.float32)).astype(ml_dtypes.bfloat16)
    ones = np.ones((1, LANES))
    window_re = (cos_tab.sum(1)[:, None] * ones).astype(np.float32)
    window_im = (-sin_tab.sum(1)[:, None] * ones).astype(np.float32)
    return np.concatenate([high, low], 0), np.stack([window_re, window_im], 0)


def turned(z, even):
    return jnp.where(even, pltpu.roll(z, 7, 0), -pltpu.roll(z, 1, 0))


def cholesky(gram_re, gram_im):
    up_re, up_im, diag_inv = {}, {}, {}
    for j in range(NB):
        pivot = gram_re[j, j]
        for k in range(j):
            pivot = pivot - (up_re[k, j] * up_re[k, j] + up_im[k, j] * up_im[k, j])
        inv = lax.rsqrt(pivot)
        inv = inv * (1.5 - 0.5 * ((pivot * inv) * inv))
        diag_inv[j] = inv
        up_re[j, j] = pivot * inv
        for i in range(j + 1, NB):
            acc_re, acc_im = gram_re[j, i], gram_im[j, i]
            for k in range(j):
                acc_re = acc_re - (up_re[k, j] * up_re[k, i] + up_im[k, j] * up_im[k, i])
                acc_im = acc_im - (up_re[k, j] * up_im[k, i] - up_im[k, j] * up_re[k, i])
            up_re[j, i] = acc_re * inv
            up_im[j, i] = acc_im * inv
    inv_re, inv_im = {}, {}
    for j in range(NB):
        inv_re[j, j] = diag_inv[j]
        for i in range(j - 1, -1, -1):
            acc_re = up_re[i, j] * inv_re[j, j]
            acc_im = up_im[i, j] * inv_re[j, j]
            for k in range(i + 1, j):
                acc_re = acc_re + up_re[i, k] * inv_re[k, j] - up_im[i, k] * inv_im[k, j]
                acc_im = acc_im + up_re[i, k] * inv_im[k, j] + up_im[i, k] * inv_re[k, j]
            inv_re[i, j] = -acc_re * diag_inv[i]
            inv_im[i, j] = -acc_im * diag_inv[i]
    return up_re, up_im, inv_re, inv_im


def kernel(
    point_total, x_hbm, w_hbm, tab_hbm, win_hbm, modes, factor_ref,
    xs, tab, win, wgt, wgt2, spec, sums, sums_in, mean_part, mean, recv, turn, prod, acc, inverse,
    share, core_in, half, space_in,
    x_sem, in_sem, send_sem, recv_sem, sums_sem, mean_sem, small_sem, core_sem, space_sem,
):
    tm = lax.axis_index("tm")
    sp = lax.axis_index("space")
    points = xs.shape[0]
    rows = 2 * points
    steps = points // 4
    per = KF // NB

    z_hi, y, core = lax.div(sp, 8), lax.rem(lax.div(sp, 2), 4), lax.rem(sp, 2)
    mates = [lax.rem(tm + d, NB) for d in range(1, NB)]
    core_peer = z_hi * 8 + y * 2 + (1 - core)
    space_peers = [
        lax.rem(z_hi + dz, 4) * 8 + lax.rem(y + dy, 4) * 2 + core
        for dz in range(4)
        for dy in range(4)
        if (dz, dy) != (0, 0)
    ]

    def x_copy(pt):
        return pltpu.make_async_copy(x_hbm.at[:, pt], xs.at[pt], x_sem.at[pt // 4])

    tab_copy = pltpu.make_async_copy(tab_hbm, tab, in_sem.at[0])
    win_copy = pltpu.make_async_copy(win_hbm, win, in_sem.at[1])
    wgt_copy = pltpu.make_async_copy(w_hbm, wgt, in_sem.at[2])
    for pt in range(4):
        x_copy(pt).start()
    tab_copy.start()
    win_copy.start()
    for pt in range(4, points):
        x_copy(pt).start()
    wgt_copy.start()

    barrier = pltpu.get_barrier_semaphore()
    for mate in mates:
        pl.semaphore_signal(barrier, 1, device_id=(mate, sp), device_id_type=MESH)
    for peer in [core_peer, *space_peers]:
        pl.semaphore_signal(barrier, 1, device_id=(tm, peer), device_id_type=MESH)

    row8 = lax.broadcasted_iota(jnp.int32, (8, LANES), 0)
    lane8 = lax.broadcasted_iota(jnp.int32, (8, LANES), 1)
    even = lax.rem(row8, 2) == 0
    spec_rows = spec.reshape(KF * rows, LANES)

    def remote(src, dst, recv_at, mate=None, peer=None, sent=None):
        return pltpu.make_async_remote_copy(
            src, dst, send_sem if sent is None else sent, recv_at,
            device_id=(tm if mate is None else mate, sp if peer is None else peer), device_id_type=MESH,
        )

    def transform_step(q):
        pltpu.make_async_copy(xs.at[pl.ds(4 * q, 4)], xs.at[pl.ds(4 * q, 4)], x_sem.at[q]).wait()
        highs, lows, bases = [], [], []
        totals = None
        for i in range(4):
            v = xs.at[4 * q + i].reshape(2 * NFFT, LANES)[...]
            base = v[0:8]
            base = base + pltpu.roll(base, 4, 0)
            base = (base + pltpu.roll(base, 2, 0)) * 0.25
            d = v.reshape(NFFT // 4, 8, LANES) - base[None]
            total = jnp.sum(d, axis=0)
            total = total + pltpu.roll(total, 4, 0)
            total = total + pltpu.roll(total, 2, 0) + base * NFFT
            totals = total if i == 0 else jnp.where(lax.div(row8, 2) == i, total, totals)
            d = d.reshape(2 * NFFT, LANES)
            high = d.astype(jnp.bfloat16)
            highs.append(high)
            lows.append((d - high.astype(jnp.float32)).astype(jnp.bfloat16))
            bases.append(base)
        both = jnp.dot(tab[...], jnp.concatenate(highs, 1), preferred_element_type=jnp.float32)
        rest = jnp.dot(tab[: 2 * KF], jnp.concatenate(lows, 1), preferred_element_type=jnp.float32)
        out = both[: 2 * KF] + both[2 * KF :] + rest
        for i in range(4):
            at = slice(i * LANES, (i + 1) * LANES)
            base_re, base_im = bases[i][0:1], bases[i][1:2]
            spec_rows[pl.ds(8 * q + 2 * i, KF, stride=rows), :] = (
                out[:KF, at] + (win[0] * base_re - win[1] * base_im)
            )
            spec_rows[pl.ds(8 * q + 2 * i + 1, KF, stride=rows), :] = (
                out[KF:, at] + (win[0] * base_im + win[1] * base_re)
            )
        sums[pl.ds(pl.multiple_of(8 * q, 8), 8), :] = totals

    def early_sends(q):
        at = pl.ds(pl.multiple_of(8 * q, 8), 8)
        for mate in mates:
            remote(
                spec.at[mate, pl.ds(0, EARLY), at], recv.at[pl.ds(0, EARLY), tm, at], recv_sem.at[0], mate=mate
            ).start()

    tab_copy.wait()
    win_copy.wait()
    transform_step(0)
    pl.semaphore_wait(barrier, len(mates) + 1 + len(space_peers))
    early_sends(0)

    @pl.loop(1, steps)
    def _(q):
        transform_step(q)
        early_sends(q)

    pltpu.make_async_copy(spec.at[tm, pl.ds(0, EARLY)], recv.at[pl.ds(0, EARLY), tm], recv_sem.at[0]).start()
    for mate in mates:
        remote(
            sums.at[pl.ds(pl.multiple_of(8 * mate, 8), 8)], sums_in.at[tm], sums_sem, mate=mate, sent=small_sem.at[0]
        ).start()
    pltpu.make_async_copy(sums.at[pl.ds(pl.multiple_of(8 * tm, 8), 8)], sums_in.at[tm], sums_sem).start()
    def sends(f):
        for mate in mates:
            remote(spec.at[mate, f], recv.at[f, tm], recv_sem.at[f], mate=mate).start()
        pltpu.make_async_copy(spec.at[tm, f], recv.at[f, tm], recv_sem.at[f]).start()

    for f in range(EARLY, FILL):
        sends(f)

    pltpu.make_async_copy(sums_in, sums_in, sums_sem).wait()
    part = sums_in[0]
    for a in range(1, NB):
        part = part + sums_in[a]
    mean_part[...] = part * (1.0 / (NB * NFFT))
    for mate in mates:
        remote(mean_part, mean.at[tm], mean_sem, mate=mate, sent=small_sem.at[1]).start()
    pltpu.make_async_copy(mean_part, mean.at[tm], mean_sem).start()
    for f in range(FILL, WINDOW):
        sends(f)
    wgt_copy.wait()
    scaled = wgt[...] / point_total
    wgt2[pl.ds(0, points, stride=2), :] = scaled
    wgt2[pl.ds(1, points, stride=2), :] = scaled
    pltpu.make_async_copy(mean, mean, mean_sem).wait()

    groups = rows // 8

    def gram_step(f, total):
        win_re = jnp.broadcast_to(win[0, pl.ds(per * tm + f, 1), :], (8, LANES))
        win_im = jnp.broadcast_to(win[1, pl.ds(per * tm + f, 1), :], (8, LANES))
        for g in range(groups):
            at = pl.ds(8 * g, 8)
            m = mean[g]
            shift = win_re * m - win_im * turned(m, even)
            weight = wgt2[at, :]
            for a in range(NB):
                z = recv[f, a, at, :] - shift
                recv[f, a, at, :] = z
                turn[f, a, at, :] = turned(z, even)
                prod[a, at, :] = z * weight
        for a in range(NB):
            sums_re = {}
            sums_im = {}
            for g in range(groups):
                at = pl.ds(8 * g, 8)
                p = prod[a, at, :]
                for b in range(a, NB):
                    term = p * recv[f, b, at, :]
                    sums_re[b] = term if g == 0 else sums_re[b] + term
                    if b > a:
                        term = p * turn[f, b, at, :]
                        sums_im[b] = term if g == 0 else sums_im[b] + term
            for b in range(a, NB):
                acc[pl.ds(8 * SLOT_RE[a, b], 8), :] = sums_re[b]
                if b > a:
                    acc[pl.ds(8 * SLOT_IM[a, b], 8), :] = sums_im[b]
        folded = acc[pl.ds(0, SLOTS, stride=8), :]
        for s in range(1, 8):
            folded = folded + acc[pl.ds(s, SLOTS, stride=8), :]
        folded = jnp.concatenate([folded, jnp.zeros((LANES - SLOTS, LANES), jnp.float32)], 0)
        line = lax.dot_general(
            jnp.ones((8, LANES), jnp.float32), folded, (((1,), (1,)), ((), ())),
            precision=lax.Precision.HIGHEST, preferred_element_type=jnp.float32,
        )
        return jnp.where(row8 == f, line, total)

    def core_start(n, total):
        share[n] = total
        remote(share.at[n], core_in.at[n], core_sem.at[n, 0], peer=core_peer, sent=core_sem.at[n, 1]).start()

    def space_start(n):
        pltpu.make_async_copy(core_in.at[n], core_in.at[n], core_sem.at[n, 0]).wait()
        half[n] = share[n] + core_in[n]
        for i, peer in enumerate(space_peers):
            remote(half.at[n], space_in.at[n, i], space_sem.at[n, 0], peer=peer, sent=space_sem.at[n, 1]).start()

    def factored(n):
        pltpu.make_async_copy(space_in.at[n], space_in.at[n], space_sem.at[n, 0]).wait()
        terms = [half[n]] + [space_in[n, i] for i in range(len(space_peers))]
        while len(terms) > 1:
            terms = [a + b for a, b in zip(terms[::2], terms[1::2])]
        gram = terms[0]
        spread = [jnp.broadcast_to(gram[:, i : i + 1], (8, LANES)) for i in range(SLOTS)]
        gram_re = {pair: spread[SLOT_RE[pair]] for pair in PAIRS_RE}
        gram_im = {pair: spread[SLOT_IM[pair]] for pair in PAIRS_IM}
        zero = jnp.zeros((8, LANES), jnp.float32)
        up_re, up_im, inv_re, inv_im = cholesky(
            gram_re, {**gram_im, **{(j, j): zero for j in range(NB)}}
        )
        for pair in PAIRS_RE:
            inverse[SLOT_RE[pair]] = inv_re[pair]
        for pair in PAIRS_IM:
            inverse[SLOT_IM[pair]] = inv_im[pair]
        lines = zero
        for a, b in PAIRS_RE:
            lines = jnp.where(lane8 == (NB - 1 - a) * NB + b, up_re[a, b], lines)
        for a, b in PAIRS_IM:
            lines = jnp.where(lane8 == NB * NB + (NB - 1 - a) * NB + b, up_im[a, b], lines)
        return lines

    def apply_step(f):
        co_re = {p: jnp.broadcast_to(inverse[SLOT_RE[p], pl.ds(f, 1), :], (8, LANES)) for p in PAIRS_RE}
        co_im = {p: jnp.broadcast_to(inverse[SLOT_IM[p], pl.ds(f, 1), :], (8, LANES)) for p in PAIRS_IM}
        for b in range(NB):
            for g in range(groups):
                at = pl.ds(8 * g, 8)
                total = recv[f, 0, at, :] * co_re[0, b]
                for a in range(1, b + 1):
                    total = total + recv[f, a, at, :] * co_re[a, b]
                for a in range(b):
                    total = total - turn[f, a, at, :] * co_im[a, b]
                modes[b, f, at, :] = total

    pltpu.make_async_copy(recv.at[pl.ds(0, EARLY)], recv.at[pl.ds(0, EARLY)], recv_sem.at[0]).wait()
    def spectrum_step(f, total):
        @pl.when(f >= EARLY)
        def _():
            pltpu.make_async_copy(recv.at[f], recv.at[f], recv_sem.at[f]).wait()

        @pl.when(f + WINDOW < per)
        def _():
            sends(f + WINDOW)

        total = gram_step(f, total)

        @pl.when(f == SPLIT - 1)
        def _():
            core_start(0, total)

        @pl.when(f == SPLIT)
        def _():
            space_start(0)

        return total

    total = lax.fori_loop(0, per, spectrum_step, jnp.zeros((8, LANES), jnp.float32))
    core_start(1, total)
    space_start(1)
    factored(0)
    pl.loop(0, SPLIT)(apply_step)
    factor = factored(1)
    pl.loop(SPLIT, per)(apply_step)
    for f in range(per):
        line = jnp.broadcast_to(factor[f : f + 1], (8, LANES))
        for c in range(2):
            upper_half = line if c == 1 else pltpu.roll(line, LANES // 2, 1)
            factor_ref[f, c] = pltpu.roll(upper_half, NB, 1, stride=NB, stride_axis=0)[:, :NB]

    sent = spec.at[pl.ds(0, NB - 1)]
    pltpu.make_async_copy(sent, sent, send_sem).wait()
    sent = sums_in.at[pl.ds(0, NB - 1)]
    for i in range(2):
        pltpu.make_async_copy(sent, sent, small_sem.at[i]).wait()
        pltpu.make_async_copy(core_in.at[i], core_in.at[i], core_sem.at[i, 1]).wait()
        pltpu.make_async_copy(space_in.at[i], space_in.at[i], space_sem.at[i, 1]).wait()


def body(snapshots, quad_weights):
    cell_count = snapshots.shape[2]
    points = cell_count // LANES
    rows = 2 * points
    per = KF // NB
    point_total = cell_count * lax.axis_size("space")
    others = lax.axis_size("space") // 2 - 1
    x = snapshots.reshape(NFFT, 2, points, LANES).transpose(0, 2, 1, 3)
    tab, win = tables()
    operands = (x, quad_weights.reshape(points, LANES), jnp.asarray(tab), jnp.asarray(win))
    f32 = jnp.float32
    in_hbm = pl.BlockSpec(memory_space=pltpu.HBM)
    in_vmem = pl.BlockSpec(memory_space=pltpu.VMEM)
    dma = pltpu.SemaphoreType.DMA
    modes, factor = pl.pallas_call(
        functools.partial(kernel, point_total),
        out_shape=(
            jax.ShapeDtypeStruct((NB, per, rows, LANES), f32),
            jax.ShapeDtypeStruct((per, 2, NB, NB), f32),
        ),
        in_specs=[in_hbm] * 4,
        out_specs=(in_vmem, in_vmem),
        scratch_shapes=[
            pltpu.VMEM((points, NFFT, 2, LANES), f32),
            pltpu.VMEM((4 * KF, 2 * NFFT), jnp.bfloat16),
            pltpu.VMEM((2, KF, LANES), f32),
            pltpu.VMEM((points, LANES), f32),
            pltpu.VMEM((rows, LANES), f32),
            pltpu.VMEM((NB, per, rows, LANES), f32),
            pltpu.VMEM((rows, LANES), f32),
            pltpu.VMEM((NB, 8, LANES), f32),
            pltpu.VMEM((8, LANES), f32),
            pltpu.VMEM((NB, 8, LANES), f32),
            pltpu.VMEM((per, NB, rows, LANES), f32),
            pltpu.VMEM((per, NB, rows, LANES), f32),
            pltpu.VMEM((NB, rows, LANES), f32),
            pltpu.VMEM((SLOTS * 8, LANES), f32),
            pltpu.VMEM((SLOTS, 8, LANES), f32),
            pltpu.VMEM((2, 8, LANES), f32),
            pltpu.VMEM((2, 8, LANES), f32),
            pltpu.VMEM((2, 8, LANES), f32),
            pltpu.VMEM((2, others, 8, LANES), f32),
            dma((points // 4,)),
            dma((3,)),
            dma,
            dma((per,)),
            dma,
            dma,
            dma((2,)),
            dma((2, 2)),
            dma((2, 2)),
        ],
        compiler_params=pltpu.CompilerParams(
            collective_id=0, has_side_effects=True, vmem_limit_bytes=48 * 2**20
        ),
    )(*(pltpu.with_memory_space_constraint(v, pltpu.HBM) for v in operands))
    modes = modes.reshape(NB, per, points, 2, LANES).transpose(0, 1, 3, 2, 4)
    return (modes.reshape(NB, per, 2, cell_count), factor)


def solution(mesh):
    placed = (P("tm", None, "space"), P("space"))
    return jax.shard_map(
        body,
        mesh=mesh,
        in_specs=placed,
        out_specs=(P(None, "tm", None, "space"), P("tm", None, None, None)),
        check_vma=False,
    )
```

```python
import functools
import math

import jax
import jax.numpy as jnp
import ml_dtypes
import numpy as np
from jax import lax
from jax.experimental import pallas as pl
from jax.experimental.pallas import tpu as pltpu
from jax.sharding import PartitionSpec as P

NB = 8
NFFT = 256
KF = 64
LANES = 128
EARLY = 3
SPLIT = 6
FILL = 4
WINDOW = 8
MESH = pl.DeviceIdType.MESH

PAIRS_RE = [(a, b) for a in range(NB) for b in range(a, NB)]
PAIRS_IM = [(a, b) for a in range(NB) for b in range(a + 1, NB)]
SLOT_RE = {pair: i for i, pair in enumerate(PAIRS_RE)}
SLOT_IM = {pair: len(PAIRS_RE) + i for i, pair in enumerate(PAIRS_IM)}
SLOTS = len(PAIRS_RE) + len(PAIRS_IM)


def tables():
    j = np.arange(NFFT)
    k = np.arange(KF)
    window = 0.54 - 0.46 * np.cos(2.0 * math.pi * j / NFFT)
    angles = 2.0 * math.pi * (k[:, None] * j[None, :] % NFFT) / NFFT
    cos_tab = window * np.cos(angles)
    sin_tab = window * np.sin(angles)
    full = np.zeros((2, KF, NFFT, 2))
    full[0, :, :, 0] = cos_tab
    full[0, :, :, 1] = sin_tab
    full[1, :, :, 0] = -sin_tab
    full[1, :, :, 1] = cos_tab
    full = full.reshape(2 * KF, 2 * NFFT).astype(np.float32)
    high = full.astype(ml_dtypes.bfloat16)
    low = (full - high.astype(np.float32)).astype(ml_dtypes.bfloat16)
    ones = np.ones((1, LANES))
    window_re = (cos_tab.sum(1)[:, None] * ones).astype(np.float32)
    window_im = (-sin_tab.sum(1)[:, None] * ones).astype(np.float32)
    return np.concatenate([high, low], 0), np.stack([window_re, window_im], 0)


def turned(z, even):
    return jnp.where(even, pltpu.roll(z, 7, 0), -pltpu.roll(z, 1, 0))


def cholesky(gram_re, gram_im):
    up_re, up_im, diag_inv = {}, {}, {}
    for j in range(NB):
        pivot = gram_re[j, j]
        for k in range(j):
            pivot = pivot - (up_re[k, j] * up_re[k, j] + up_im[k, j] * up_im[k, j])
        inv = lax.rsqrt(pivot)
        inv = inv * (1.5 - 0.5 * ((pivot * inv) * inv))
        diag_inv[j] = inv
        up_re[j, j] = pivot * inv
        for i in range(j + 1, NB):
            acc_re, acc_im = gram_re[j, i], gram_im[j, i]
            for k in range(j):
                acc_re = acc_re - (up_re[k, j] * up_re[k, i] + up_im[k, j] * up_im[k, i])
                acc_im = acc_im - (up_re[k, j] * up_im[k, i] - up_im[k, j] * up_re[k, i])
            up_re[j, i] = acc_re * inv
            up_im[j, i] = acc_im * inv
    inv_re, inv_im = {}, {}
    for j in range(NB):
        inv_re[j, j] = diag_inv[j]
        for i in range(j - 1, -1, -1):
            acc_re = up_re[i, j] * inv_re[j, j]
            acc_im = up_im[i, j] * inv_re[j, j]
            for k in range(i + 1, j):
                acc_re = acc_re + up_re[i, k] * inv_re[k, j] - up_im[i, k] * inv_im[k, j]
                acc_im = acc_im + up_re[i, k] * inv_im[k, j] + up_im[i, k] * inv_re[k, j]
            inv_re[i, j] = -acc_re * diag_inv[i]
            inv_im[i, j] = -acc_im * diag_inv[i]
    return up_re, up_im, inv_re, inv_im


def kernel(
    point_total, x_hbm, w_hbm, tab_hbm, win_hbm, modes, factor_ref,
    xs, tab, win, wgt, wgt2, spec, sums, sums_in, mean_part, mean, recv, turn, prod, acc, inverse,
    share, core_in, half, space_in,
    x_sem, in_sem, send_sem, recv_sem, sums_sem, mean_sem, small_sem, core_sem, space_sem,
):
    tm = lax.axis_index("tm")
    sp = lax.axis_index("space")
    points = xs.shape[0]
    rows = 2 * points
    steps = points // 4
    per = KF // NB

    z_hi, y, core = lax.div(sp, 8), lax.rem(lax.div(sp, 2), 4), lax.rem(sp, 2)
    mates = [lax.rem(tm + d, NB) for d in range(1, NB)]
    core_peer = z_hi * 8 + y * 2 + (1 - core)
    around = [(dz, dy) for dz in range(4) for dy in range(4) if (dz, dy) != (0, 0)]
    around.sort(key=lambda way: -2 * min(way[0], 4 - way[0]) - min(way[1], 4 - way[1]))
    space_peers = [
        lax.rem(z_hi + dz, 4) * 8 + lax.rem(y + dy, 4) * 2 + core for dz, dy in around
    ]

    def x_copy(pt):
        return pltpu.make_async_copy(x_hbm.at[:, pt], xs.at[pt], x_sem.at[pt // 4])

    barrier = pltpu.get_barrier_semaphore()
    for peer in [*space_peers, core_peer]:
        pl.semaphore_signal(barrier, 1, device_id=(tm, peer), device_id_type=MESH)
    for mate in mates:
        pl.semaphore_signal(barrier, 1, device_id=(mate, sp), device_id_type=MESH)

    tab_copy = pltpu.make_async_copy(tab_hbm, tab, in_sem.at[0])
    win_copy = pltpu.make_async_copy(win_hbm, win, in_sem.at[1])
    wgt_copy = pltpu.make_async_copy(w_hbm, wgt, in_sem.at[2])
    for pt in range(4):
        x_copy(pt).start()
    tab_copy.start()
    win_copy.start()
    for pt in range(4, points):
        x_copy(pt).start()
    wgt_copy.start()

    row8 = lax.broadcasted_iota(jnp.int32, (8, LANES), 0)
    lane8 = lax.broadcasted_iota(jnp.int32, (8, LANES), 1)
    even = lax.rem(row8, 2) == 0
    spec_rows = spec.reshape(KF * rows, LANES)

    def remote(src, dst, recv_at, mate=None, peer=None, sent=None):
        return pltpu.make_async_remote_copy(
            src, dst, send_sem if sent is None else sent, recv_at,
            device_id=(tm if mate is None else mate, sp if peer is None else peer), device_id_type=MESH,
        )

    def transform_step(q):
        pltpu.make_async_copy(xs.at[pl.ds(4 * q, 4)], xs.at[pl.ds(4 * q, 4)], x_sem.at[q]).wait()
        highs, lows, bases = [], [], []
        totals = None
        for i in range(4):
            v = xs.at[4 * q + i].reshape(2 * NFFT, LANES)[...]
            base = v[0:8]
            base = base + pltpu.roll(base, 4, 0)
            base = (base + pltpu.roll(base, 2, 0)) * 0.25
            d = v.reshape(NFFT // 4, 8, LANES) - base[None]
            total = jnp.sum(d, axis=0)
            total = total + pltpu.roll(total, 4, 0)
            total = total + pltpu.roll(total, 2, 0) + base * NFFT
            totals = total if i == 0 else jnp.where(lax.div(row8, 2) == i, total, totals)
            d = d.reshape(2 * NFFT, LANES)
            high = d.astype(jnp.bfloat16)
            highs.append(high)
            lows.append((d - high.astype(jnp.float32)).astype(jnp.bfloat16))
            bases.append(base)
        both = jnp.dot(tab[...], jnp.concatenate(highs, 1), preferred_element_type=jnp.float32)
        rest = jnp.dot(tab[: 2 * KF], jnp.concatenate(lows, 1), preferred_element_type=jnp.float32)
        out = both[: 2 * KF] + both[2 * KF :] + rest
        for i in range(4):
            at = slice(i * LANES, (i + 1) * LANES)
            base_re, base_im = bases[i][0:1], bases[i][1:2]
            spec_rows[pl.ds(8 * q + 2 * i, KF, stride=rows), :] = (
                out[:KF, at] + (win[0] * base_re - win[1] * base_im)
            )
            spec_rows[pl.ds(8 * q + 2 * i + 1, KF, stride=rows), :] = (
                out[KF:, at] + (win[0] * base_im + win[1] * base_re)
            )
        sums[pl.ds(pl.multiple_of(8 * q, 8), 8), :] = totals

    def early_sends(q):
        at = pl.ds(pl.multiple_of(8 * q, 8), 8)
        for mate in mates:
            remote(
                spec.at[mate, pl.ds(0, EARLY), at], recv.at[pl.ds(0, EARLY), tm, at], recv_sem.at[0], mate=mate
            ).start()

    def sums_send(q):
        part = sums.at[pl.ds(pl.multiple_of(8 * q, 8), 8)]

        @pl.when(tm != q)
        def _():
            remote(part, sums_in.at[tm], sums_sem, mate=q, sent=small_sem.at[0]).start()

        @pl.when(tm == q)
        def _():
            pltpu.make_async_copy(part, sums_in.at[tm], sums_sem).start()

    tab_copy.wait()
    win_copy.wait()
    transform_step(0)
    pl.semaphore_wait(barrier, len(mates) + 1 + len(space_peers))
    sums_send(0)
    early_sends(0)

    @pl.loop(1, steps)
    def _(q):
        transform_step(q)
        sums_send(q)
        early_sends(q)

    pltpu.make_async_copy(spec.at[tm, pl.ds(0, EARLY)], recv.at[pl.ds(0, EARLY), tm], recv_sem.at[0]).start()
    def sends(f):
        for mate in mates:
            remote(spec.at[mate, f], recv.at[f, tm], recv_sem.at[f], mate=mate).start()
        pltpu.make_async_copy(spec.at[tm, f], recv.at[f, tm], recv_sem.at[f]).start()

    for f in range(EARLY, FILL):
        sends(f)

    pltpu.make_async_copy(sums_in, sums_in, sums_sem).wait()
    part = sums_in[0]
    for a in range(1, NB):
        part = part + sums_in[a]
    mean_part[...] = part * (1.0 / (NB * NFFT))
    for mate in mates:
        remote(mean_part, mean.at[tm], mean_sem, mate=mate, sent=small_sem.at[1]).start()
    pltpu.make_async_copy(mean_part, mean.at[tm], mean_sem).start()
    for f in range(FILL, WINDOW):
        sends(f)
    wgt_copy.wait()
    scaled = wgt[...] / point_total
    wgt2[pl.ds(0, points, stride=2), :] = scaled
    wgt2[pl.ds(1, points, stride=2), :] = scaled
    pltpu.make_async_copy(mean, mean, mean_sem).wait()

    groups = rows // 8

    def gram_step(f, total):
        win_re = jnp.broadcast_to(win[0, pl.ds(per * tm + f, 1), :], (8, LANES))
        win_im = jnp.broadcast_to(win[1, pl.ds(per * tm + f, 1), :], (8, LANES))
        for g in range(groups):
            at = pl.ds(8 * g, 8)
            m = mean[g]
            shift = win_re * m - win_im * turned(m, even)
            weight = wgt2[at, :]
            for a in range(NB):
                z = recv[f, a, at, :] - shift
                recv[f, a, at, :] = z
                turn[f, a, at, :] = turned(z, even)
                prod[a, at, :] = z * weight
        for a in range(NB):
            sums_re = {}
            sums_im = {}
            for g in range(groups):
                at = pl.ds(8 * g, 8)
                p = prod[a, at, :]
                for b in range(a, NB):
                    term = p * recv[f, b, at, :]
                    sums_re[b] = term if g == 0 else sums_re[b] + term
                    if b > a:
                        term = p * turn[f, b, at, :]
                        sums_im[b] = term if g == 0 else sums_im[b] + term
            for b in range(a, NB):
                acc[pl.ds(8 * SLOT_RE[a, b], 8), :] = sums_re[b]
                if b > a:
                    acc[pl.ds(8 * SLOT_IM[a, b], 8), :] = sums_im[b]
        folded = acc[pl.ds(0, SLOTS, stride=8), :]
        for s in range(1, 8):
            folded = folded + acc[pl.ds(s, SLOTS, stride=8), :]
        folded = jnp.concatenate([folded, jnp.zeros((LANES - SLOTS, LANES), jnp.float32)], 0)
        line = lax.dot_general(
            jnp.ones((8, LANES), jnp.float32), folded, (((1,), (1,)), ((), ())),
            precision=lax.Precision.HIGHEST, preferred_element_type=jnp.float32,
        )
        return jnp.where(row8 == f, line, total)

    def core_start(n, total):
        share[n] = total
        remote(share.at[n], core_in.at[n], core_sem.at[n, 0], peer=core_peer, sent=core_sem.at[n, 1]).start()

    def space_start(n):
        pltpu.make_async_copy(core_in.at[n], core_in.at[n], core_sem.at[n, 0]).wait()
        half[n] = share[n] + core_in[n]
        for i, peer in enumerate(space_peers):
            remote(half.at[n], space_in.at[n, i], space_sem.at[n, 0], peer=peer, sent=space_sem.at[n, 1]).start()

    def factored(n):
        pltpu.make_async_copy(space_in.at[n], space_in.at[n], space_sem.at[n, 0]).wait()
        terms = [half[n]] + [space_in[n, i] for i in range(len(space_peers))]
        while len(terms) > 1:
            terms = [a + b for a, b in zip(terms[::2], terms[1::2])]
        gram = terms[0]
        spread = [jnp.broadcast_to(gram[:, i : i + 1], (8, LANES)) for i in range(SLOTS)]
        gram_re = {pair: spread[SLOT_RE[pair]] for pair in PAIRS_RE}
        gram_im = {pair: spread[SLOT_IM[pair]] for pair in PAIRS_IM}
        zero = jnp.zeros((8, LANES), jnp.float32)
        up_re, up_im, inv_re, inv_im = cholesky(
            gram_re, {**gram_im, **{(j, j): zero for j in range(NB)}}
        )
        for pair in PAIRS_RE:
            inverse[SLOT_RE[pair]] = inv_re[pair]
        for pair in PAIRS_IM:
            inverse[SLOT_IM[pair]] = inv_im[pair]
        lines = zero
        for a, b in PAIRS_RE:
            lines = jnp.where(lane8 == (NB - 1 - a) * NB + b, up_re[a, b], lines)
        for a, b in PAIRS_IM:
            lines = jnp.where(lane8 == NB * NB + (NB - 1 - a) * NB + b, up_im[a, b], lines)
        return lines

    def apply_step(f):
        co_re = {p: jnp.broadcast_to(inverse[SLOT_RE[p], pl.ds(f, 1), :], (8, LANES)) for p in PAIRS_RE}
        co_im = {p: jnp.broadcast_to(inverse[SLOT_IM[p], pl.ds(f, 1), :], (8, LANES)) for p in PAIRS_IM}
        for b in range(NB):
            for g in range(groups):
                at = pl.ds(8 * g, 8)
                total = recv[f, 0, at, :] * co_re[0, b]
                for a in range(1, b + 1):
                    total = total + recv[f, a, at, :] * co_re[a, b]
                for a in range(b):
                    total = total - turn[f, a, at, :] * co_im[a, b]
                modes[b, f, at, :] = total

    pltpu.make_async_copy(recv.at[pl.ds(0, EARLY)], recv.at[pl.ds(0, EARLY)], recv_sem.at[0]).wait()
    def spectrum_step(f, total):
        @pl.when(f >= EARLY)
        def _():
            pltpu.make_async_copy(recv.at[f], recv.at[f], recv_sem.at[f]).wait()

        @pl.when(f + WINDOW < per)
        def _():
            sends(f + WINDOW)

        total = gram_step(f, total)

        @pl.when(f == SPLIT - 1)
        def _():
            core_start(0, total)

        @pl.when(f == SPLIT)
        def _():
            space_start(0)

        return total

    total = lax.fori_loop(0, per, spectrum_step, jnp.zeros((8, LANES), jnp.float32))
    core_start(1, total)
    space_start(1)
    factored(0)
    pl.loop(0, SPLIT)(apply_step)
    factor = factored(1)
    pl.loop(SPLIT, per)(apply_step)
    for f in range(per):
        line = jnp.broadcast_to(factor[f : f + 1], (8, LANES))
        for c in range(2):
            upper_half = line if c == 1 else pltpu.roll(line, LANES // 2, 1)
            factor_ref[f, c] = pltpu.roll(upper_half, NB, 1, stride=NB, stride_axis=0)[:, :NB]

    sent = spec.at[pl.ds(0, NB - 1)]
    pltpu.make_async_copy(sent, sent, send_sem).wait()
    sent = sums_in.at[pl.ds(0, NB - 1)]
    for i in range(2):
        pltpu.make_async_copy(sent, sent, small_sem.at[i]).wait()
        pltpu.make_async_copy(core_in.at[i], core_in.at[i], core_sem.at[i, 1]).wait()
        pltpu.make_async_copy(space_in.at[i], space_in.at[i], space_sem.at[i, 1]).wait()


def writer(modes, factor, modes_out, factor_out, sem):
    copies = [pltpu.make_async_copy(modes.at[b], modes_out.at[b], sem.at[b]) for b in range(NB)]
    copies.append(pltpu.make_async_copy(factor, factor_out, sem.at[NB]))
    for copy in copies:
        copy.start()
    for copy in copies:
        copy.wait()


def body(snapshots, quad_weights):
    cell_count = snapshots.shape[2]
    points = cell_count // LANES
    rows = 2 * points
    per = KF // NB
    point_total = cell_count * lax.axis_size("space")
    others = lax.axis_size("space") // 2 - 1
    x = snapshots.reshape(NFFT, 2, points, LANES).transpose(0, 2, 1, 3)
    tab, win = tables()
    operands = (x, quad_weights.reshape(points, LANES), jnp.asarray(tab), jnp.asarray(win))
    f32 = jnp.float32
    in_hbm = pl.BlockSpec(memory_space=pltpu.HBM)
    in_vmem = pl.BlockSpec(memory_space=pltpu.VMEM)
    dma = pltpu.SemaphoreType.DMA
    modes, factor = pl.pallas_call(
        functools.partial(kernel, point_total),
        out_shape=(
            jax.ShapeDtypeStruct((NB, per, rows, LANES), f32),
            jax.ShapeDtypeStruct((per, 2, NB, NB), f32),
        ),
        in_specs=[in_hbm] * 4,
        out_specs=(in_vmem, in_vmem),
        scratch_shapes=[
            pltpu.VMEM((points, NFFT, 2, LANES), f32),
            pltpu.VMEM((4 * KF, 2 * NFFT), jnp.bfloat16),
            pltpu.VMEM((2, KF, LANES), f32),
            pltpu.VMEM((points, LANES), f32),
            pltpu.VMEM((rows, LANES), f32),
            pltpu.VMEM((NB, per, rows, LANES), f32),
            pltpu.VMEM((rows, LANES), f32),
            pltpu.VMEM((NB, 8, LANES), f32),
            pltpu.VMEM((8, LANES), f32),
            pltpu.VMEM((NB, 8, LANES), f32),
            pltpu.VMEM((per, NB, rows, LANES), f32),
            pltpu.VMEM((per, NB, rows, LANES), f32),
            pltpu.VMEM((NB, rows, LANES), f32),
            pltpu.VMEM((SLOTS * 8, LANES), f32),
            pltpu.VMEM((SLOTS, 8, LANES), f32),
            pltpu.VMEM((2, 8, LANES), f32),
            pltpu.VMEM((2, 8, LANES), f32),
            pltpu.VMEM((2, 8, LANES), f32),
            pltpu.VMEM((2, others, 8, LANES), f32),
            dma((points // 4,)),
            dma((3,)),
            dma,
            dma((per,)),
            dma,
            dma,
            dma((2,)),
            dma((2, 2)),
            dma((2, 2)),
        ],
        compiler_params=pltpu.CompilerParams(
            collective_id=0, has_side_effects=True, vmem_limit_bytes=48 * 2**20
        ),
    )(*(pltpu.with_memory_space_constraint(v, pltpu.HBM) for v in operands))
    modes, factor = pl.pallas_call(
        writer,
        out_shape=(jax.ShapeDtypeStruct(modes.shape, f32), jax.ShapeDtypeStruct(factor.shape, f32)),
        in_specs=[in_vmem] * 2,
        out_specs=(in_hbm, in_hbm),
        scratch_shapes=[dma((NB + 1,))],
        compiler_params=pltpu.CompilerParams(vmem_limit_bytes=8 * 2**20),
    )(modes, factor)
    modes = modes.reshape(NB, per, points, 2, LANES).transpose(0, 1, 3, 2, 4)
    return (modes.reshape(NB, per, 2, cell_count), factor)


def solution(mesh):
    placed = (P("tm", None, "space"), P("space"))
    return jax.shard_map(
        body,
        mesh=mesh,
        in_specs=placed,
        out_specs=(P(None, "tm", None, "space"), P("tm", None, None, None)),
        check_vma=False,
    )
```

```python
import functools
import math

import jax
import jax.numpy as jnp
import ml_dtypes
import numpy as np
from jax import lax
from jax.experimental import pallas as pl
from jax.experimental.pallas import tpu as pltpu
from jax.sharding import PartitionSpec as P

NB = 8
NFFT = 256
KF = 64
LANES = 128
EARLY = 3
SPLIT = 6
FILL = 4
WINDOW = 8
MESH = pl.DeviceIdType.MESH

PAIRS_RE = [(a, b) for a in range(NB) for b in range(a, NB)]
PAIRS_IM = [(a, b) for a in range(NB) for b in range(a + 1, NB)]
SLOT_RE = {pair: i for i, pair in enumerate(PAIRS_RE)}
SLOT_IM = {pair: len(PAIRS_RE) + i for i, pair in enumerate(PAIRS_IM)}
SLOTS = len(PAIRS_RE) + len(PAIRS_IM)


def tables():
    j = np.arange(NFFT)
    k = np.arange(KF)
    window = 0.54 - 0.46 * np.cos(2.0 * math.pi * j / NFFT)
    angles = 2.0 * math.pi * (k[:, None] * j[None, :] % NFFT) / NFFT
    cos_tab = window * np.cos(angles)
    sin_tab = window * np.sin(angles)
    full = np.zeros((2, KF, NFFT, 2))
    full[0, :, :, 0] = cos_tab
    full[0, :, :, 1] = sin_tab
    full[1, :, :, 0] = -sin_tab
    full[1, :, :, 1] = cos_tab
    full = full.reshape(2 * KF, 2 * NFFT).astype(np.float32)
    high = full.astype(ml_dtypes.bfloat16)
    low = (full - high.astype(np.float32)).astype(ml_dtypes.bfloat16)
    ones = np.ones((1, LANES))
    window_re = (cos_tab.sum(1)[:, None] * ones).astype(np.float32)
    window_im = (-sin_tab.sum(1)[:, None] * ones).astype(np.float32)
    return np.concatenate([high, low], 0), np.stack([window_re, window_im], 0)


def turned(z, even):
    return jnp.where(even, pltpu.roll(z, 7, 0), -pltpu.roll(z, 1, 0))


def cholesky(gram_re, gram_im):
    up_re, up_im, diag_inv = {}, {}, {}
    for j in range(NB):
        pivot = gram_re[j, j]
        for k in range(j):
            pivot = pivot - (up_re[k, j] * up_re[k, j] + up_im[k, j] * up_im[k, j])
        inv = lax.rsqrt(pivot)
        inv = inv * (1.5 - 0.5 * ((pivot * inv) * inv))
        diag_inv[j] = inv
        up_re[j, j] = pivot * inv
        for i in range(j + 1, NB):
            acc_re, acc_im = gram_re[j, i], gram_im[j, i]
            for k in range(j):
                acc_re = acc_re - (up_re[k, j] * up_re[k, i] + up_im[k, j] * up_im[k, i])
                acc_im = acc_im - (up_re[k, j] * up_im[k, i] - up_im[k, j] * up_re[k, i])
            up_re[j, i] = acc_re * inv
            up_im[j, i] = acc_im * inv
    inv_re, inv_im = {}, {}
    for j in range(NB):
        inv_re[j, j] = diag_inv[j]
        for i in range(j - 1, -1, -1):
            acc_re = up_re[i, j] * inv_re[j, j]
            acc_im = up_im[i, j] * inv_re[j, j]
            for k in range(i + 1, j):
                acc_re = acc_re + up_re[i, k] * inv_re[k, j] - up_im[i, k] * inv_im[k, j]
                acc_im = acc_im + up_re[i, k] * inv_im[k, j] + up_im[i, k] * inv_re[k, j]
            inv_re[i, j] = -acc_re * diag_inv[i]
            inv_im[i, j] = -acc_im * diag_inv[i]
    return up_re, up_im, inv_re, inv_im


def kernel(
    point_total, x_hbm, w_hbm, tab_hbm, win_hbm, modes, factor_ref,
    xs, tab, win, wgt, wgt2, spec, sums, sums_in, mean_part, mean, recv, turn, prod, acc, inverse,
    share_0, share_1, core_in_0, core_in_1, half_0, half_1, space_in_0, space_in_1,
    x_sem, in_sem, send_sem, recv_sem, sums_sem, mean_sem, small_sem, core_sem, space_sem,
):
    share, core_in = (share_0, share_1), (core_in_0, core_in_1)
    half, space_in = (half_0, half_1), (space_in_0, space_in_1)
    tm = lax.axis_index("tm")
    sp = lax.axis_index("space")
    points = xs.shape[0]
    rows = 2 * points
    steps = points // 4
    per = KF // NB

    z_hi, y, core = lax.div(sp, 8), lax.rem(lax.div(sp, 2), 4), lax.rem(sp, 2)
    mates = [lax.rem(tm + d, NB) for d in range(1, NB)]
    core_peer = z_hi * 8 + y * 2 + (1 - core)
    around = [(dz, dy) for dz in range(4) for dy in range(4) if (dz, dy) != (0, 0)]
    around.sort(key=lambda way: -2 * min(way[0], 4 - way[0]) - min(way[1], 4 - way[1]))
    space_peers = [
        lax.rem(z_hi + dz, 4) * 8 + lax.rem(y + dy, 4) * 2 + core for dz, dy in around
    ]

    def x_copy(pt):
        return pltpu.make_async_copy(x_hbm.at[:, pt], xs.at[pt], x_sem.at[pt // 4])

    barrier = pltpu.get_barrier_semaphore()
    for peer in [*space_peers, core_peer]:
        pl.semaphore_signal(barrier, 1, device_id=(tm, peer), device_id_type=MESH)
    for mate in mates:
        pl.semaphore_signal(barrier, 1, device_id=(mate, sp), device_id_type=MESH)

    tab_copy = pltpu.make_async_copy(tab_hbm, tab, in_sem.at[0])
    win_copy = pltpu.make_async_copy(win_hbm, win, in_sem.at[1])
    wgt_copy = pltpu.make_async_copy(w_hbm, wgt, in_sem.at[2])
    for pt in range(4):
        x_copy(pt).start()
    tab_copy.start()
    win_copy.start()
    for pt in range(4, points):
        x_copy(pt).start()
    wgt_copy.start()

    row8 = lax.broadcasted_iota(jnp.int32, (8, LANES), 0)
    lane8 = lax.broadcasted_iota(jnp.int32, (8, LANES), 1)
    even = lax.rem(row8, 2) == 0
    spec_rows = spec.reshape(KF * rows, LANES)

    def remote(src, dst, recv_at, mate=None, peer=None, sent=None):
        return pltpu.make_async_remote_copy(
            src, dst, send_sem if sent is None else sent, recv_at,
            device_id=(tm if mate is None else mate, sp if peer is None else peer), device_id_type=MESH,
        )

    def transform_step(q):
        pltpu.make_async_copy(xs.at[pl.ds(4 * q, 4)], xs.at[pl.ds(4 * q, 4)], x_sem.at[q]).wait()
        highs, lows, bases = [], [], []
        totals = None
        for i in range(4):
            v = xs.at[4 * q + i].reshape(2 * NFFT, LANES)[...]
            base = v[0:8]
            base = base + pltpu.roll(base, 4, 0)
            base = (base + pltpu.roll(base, 2, 0)) * 0.25
            d = v.reshape(NFFT // 4, 8, LANES) - base[None]
            total = jnp.sum(d, axis=0)
            total = total + pltpu.roll(total, 4, 0)
            total = total + pltpu.roll(total, 2, 0) + base * NFFT
            totals = total if i == 0 else jnp.where(lax.div(row8, 2) == i, total, totals)
            d = d.reshape(2 * NFFT, LANES)
            high = d.astype(jnp.bfloat16)
            highs.append(high)
            lows.append((d - high.astype(jnp.float32)).astype(jnp.bfloat16))
            bases.append(base)
        both = jnp.dot(tab[...], jnp.concatenate(highs, 1), preferred_element_type=jnp.float32)
        rest = jnp.dot(tab[: 2 * KF], jnp.concatenate(lows, 1), preferred_element_type=jnp.float32)
        out = both[: 2 * KF] + both[2 * KF :] + rest
        for i in range(4):
            at = slice(i * LANES, (i + 1) * LANES)
            base_re, base_im = bases[i][0:1], bases[i][1:2]
            spec_rows[pl.ds(8 * q + 2 * i, KF, stride=rows), :] = (
                out[:KF, at] + (win[0] * base_re - win[1] * base_im)
            )
            spec_rows[pl.ds(8 * q + 2 * i + 1, KF, stride=rows), :] = (
                out[KF:, at] + (win[0] * base_im + win[1] * base_re)
            )
        sums[pl.ds(pl.multiple_of(8 * q, 8), 8), :] = totals

    def early_sends(q):
        at = pl.ds(pl.multiple_of(8 * q, 8), 8)
        for mate in mates:
            remote(
                spec.at[mate, pl.ds(0, EARLY), at], recv.at[pl.ds(0, EARLY), tm, at], recv_sem.at[0], mate=mate
            ).start()

    def sums_send(q):
        part = sums.at[pl.ds(pl.multiple_of(8 * q, 8), 8)]

        @pl.when(tm != q)
        def _():
            remote(part, sums_in.at[tm], sums_sem, mate=q, sent=small_sem.at[0]).start()

        @pl.when(tm == q)
        def _():
            pltpu.make_async_copy(part, sums_in.at[tm], sums_sem).start()

    tab_copy.wait()
    win_copy.wait()
    transform_step(0)
    pl.semaphore_wait(barrier, len(mates) + 1 + len(space_peers))
    sums_send(0)
    early_sends(0)

    @pl.loop(1, steps)
    def _(q):
        transform_step(q)
        sums_send(q)
        early_sends(q)

    pltpu.make_async_copy(spec.at[tm, pl.ds(0, EARLY)], recv.at[pl.ds(0, EARLY), tm], recv_sem.at[0]).start()
    def sends(f):
        for mate in mates:
            remote(spec.at[mate, f], recv.at[f, tm], recv_sem.at[f], mate=mate).start()
        pltpu.make_async_copy(spec.at[tm, f], recv.at[f, tm], recv_sem.at[f]).start()

    for f in range(EARLY, FILL):
        sends(f)

    pltpu.make_async_copy(sums_in, sums_in, sums_sem).wait()
    part = sums_in[0]
    for a in range(1, NB):
        part = part + sums_in[a]
    mean_part[...] = part * (1.0 / (NB * NFFT))
    for mate in mates:
        remote(mean_part, mean.at[tm], mean_sem, mate=mate, sent=small_sem.at[1]).start()
    pltpu.make_async_copy(mean_part, mean.at[tm], mean_sem).start()
    for f in range(FILL, WINDOW):
        sends(f)
    wgt_copy.wait()
    scaled = wgt[...] / point_total
    wgt2[pl.ds(0, points, stride=2), :] = scaled
    wgt2[pl.ds(1, points, stride=2), :] = scaled
    pltpu.make_async_copy(mean, mean, mean_sem).wait()

    groups = rows // 8

    def gram_step(f, total):
        win_re = jnp.broadcast_to(win[0, pl.ds(per * tm + f, 1), :], (8, LANES))
        win_im = jnp.broadcast_to(win[1, pl.ds(per * tm + f, 1), :], (8, LANES))
        for g in range(groups):
            at = pl.ds(8 * g, 8)
            m = mean[g]
            shift = win_re * m - win_im * turned(m, even)
            weight = wgt2[at, :]
            for a in range(NB):
                z = recv[f, a, at, :] - shift
                recv[f, a, at, :] = z
                turn[f, a, at, :] = turned(z, even)
                prod[a, at, :] = z * weight
        for a in range(NB):
            sums_re = {}
            sums_im = {}
            for g in range(groups):
                at = pl.ds(8 * g, 8)
                p = prod[a, at, :]
                for b in range(a, NB):
                    term = p * recv[f, b, at, :]
                    sums_re[b] = term if g == 0 else sums_re[b] + term
                    if b > a:
                        term = p * turn[f, b, at, :]
                        sums_im[b] = term if g == 0 else sums_im[b] + term
            for b in range(a, NB):
                acc[pl.ds(8 * SLOT_RE[a, b], 8), :] = sums_re[b]
                if b > a:
                    acc[pl.ds(8 * SLOT_IM[a, b], 8), :] = sums_im[b]
        folded = acc[pl.ds(0, SLOTS, stride=8), :]
        for s in range(1, 8):
            folded = folded + acc[pl.ds(s, SLOTS, stride=8), :]
        folded = jnp.concatenate([folded, jnp.zeros((LANES - SLOTS, LANES), jnp.float32)], 0)
        line = lax.dot_general(
            jnp.ones((8, LANES), jnp.float32), folded, (((1,), (1,)), ((), ())),
            precision=lax.Precision.HIGHEST, preferred_element_type=jnp.float32,
        )
        return jnp.where(row8 == f, line, total)

    def core_start(n, total):
        share[n][...] = total
        remote(share[n], core_in[n], core_sem.at[n, 0], peer=core_peer, sent=core_sem.at[n, 1]).start()

    def space_start(n):
        pltpu.make_async_copy(core_in[n], core_in[n], core_sem.at[n, 0]).wait()
        half[n][...] = share[n][...] + core_in[n][...]
        for i, peer in enumerate(space_peers):
            remote(half[n], space_in[n].at[i], space_sem.at[n, 0], peer=peer, sent=space_sem.at[n, 1]).start()

    def factored(n):
        pltpu.make_async_copy(space_in[n], space_in[n], space_sem.at[n, 0]).wait()
        terms = [half[n][...]] + [space_in[n][i] for i in range(len(space_peers))]
        while len(terms) > 1:
            terms = [a + b for a, b in zip(terms[::2], terms[1::2])]
        gram = terms[0]
        if n == 1:
            gram = jnp.broadcast_to(gram, (8, LANES))
            gram = jnp.where(row8 == per - 1, pltpu.roll(gram, SLOTS, 1), gram)
        spread = [jnp.broadcast_to(gram[:, i : i + 1], (8, LANES)) for i in range(SLOTS)]
        gram_re = {pair: spread[SLOT_RE[pair]] for pair in PAIRS_RE}
        gram_im = {pair: spread[SLOT_IM[pair]] for pair in PAIRS_IM}
        zero = jnp.zeros((8, LANES), jnp.float32)
        up_re, up_im, inv_re, inv_im = cholesky(
            gram_re, {**gram_im, **{(j, j): zero for j in range(NB)}}
        )
        for pair in PAIRS_RE:
            inverse[SLOT_RE[pair]] = inv_re[pair]
        for pair in PAIRS_IM:
            inverse[SLOT_IM[pair]] = inv_im[pair]
        lines = zero
        for a, b in PAIRS_RE:
            lines = jnp.where(lane8 == (NB - 1 - a) * NB + b, up_re[a, b], lines)
        for a, b in PAIRS_IM:
            lines = jnp.where(lane8 == NB * NB + (NB - 1 - a) * NB + b, up_im[a, b], lines)
        return lines

    def apply_step(f):
        co_re = {p: jnp.broadcast_to(inverse[SLOT_RE[p], pl.ds(f, 1), :], (8, LANES)) for p in PAIRS_RE}
        co_im = {p: jnp.broadcast_to(inverse[SLOT_IM[p], pl.ds(f, 1), :], (8, LANES)) for p in PAIRS_IM}
        for b in range(NB):
            for g in range(groups):
                at = pl.ds(8 * g, 8)
                total = recv[f, 0, at, :] * co_re[0, b]
                for a in range(1, b + 1):
                    total = total + recv[f, a, at, :] * co_re[a, b]
                for a in range(b):
                    total = total - turn[f, a, at, :] * co_im[a, b]
                modes[b, f, at, :] = total

    pltpu.make_async_copy(recv.at[pl.ds(0, EARLY)], recv.at[pl.ds(0, EARLY)], recv_sem.at[0]).wait()
    def spectrum_step(f, total):
        @pl.when(f >= EARLY)
        def _():
            pltpu.make_async_copy(recv.at[f], recv.at[f], recv_sem.at[f]).wait()

        @pl.when(f + WINDOW < per)
        def _():
            sends(f + WINDOW)

        total = gram_step(f, total)

        @pl.when(f == SPLIT - 1)
        def _():
            core_start(0, total)

        @pl.when(f == SPLIT)
        def _():
            space_start(0)

        return total

    total = lax.fori_loop(0, per, spectrum_step, jnp.zeros((8, LANES), jnp.float32))
    core_start(1, total[SPLIT : SPLIT + 1] + pltpu.roll(total, SLOTS, 1)[per - 1 :])
    space_start(1)
    factor = factored(0)
    pl.loop(0, SPLIT)(apply_step)
    factor = jnp.where(row8 < SPLIT, factor, factored(1))
    pl.loop(SPLIT, per)(apply_step)
    for f in range(per):
        line = jnp.broadcast_to(factor[f : f + 1], (8, LANES))
        for c in range(2):
            upper_half = line if c == 1 else pltpu.roll(line, LANES // 2, 1)
            factor_ref[f, c] = pltpu.roll(upper_half, NB, 1, stride=NB, stride_axis=0)[:, :NB]

    sent = spec.at[pl.ds(0, NB - 1)]
    pltpu.make_async_copy(sent, sent, send_sem).wait()
    sent = sums_in.at[pl.ds(0, NB - 1)]
    for i in range(2):
        pltpu.make_async_copy(sent, sent, small_sem.at[i]).wait()
        pltpu.make_async_copy(core_in[i], core_in[i], core_sem.at[i, 1]).wait()
        pltpu.make_async_copy(space_in[i], space_in[i], space_sem.at[i, 1]).wait()


def writer(modes, factor, modes_out, factor_out, sem):
    copies = [pltpu.make_async_copy(modes.at[b], modes_out.at[b], sem.at[b]) for b in range(NB)]
    copies.append(pltpu.make_async_copy(factor, factor_out, sem.at[NB]))
    for copy in copies:
        copy.start()
    for copy in copies:
        copy.wait()


def body(snapshots, quad_weights):
    cell_count = snapshots.shape[2]
    points = cell_count // LANES
    rows = 2 * points
    per = KF // NB
    point_total = cell_count * lax.axis_size("space")
    others = lax.axis_size("space") // 2 - 1
    x = snapshots.reshape(NFFT, 2, points, LANES).transpose(0, 2, 1, 3)
    tab, win = tables()
    operands = (x, quad_weights.reshape(points, LANES), jnp.asarray(tab), jnp.asarray(win))
    f32 = jnp.float32
    in_hbm = pl.BlockSpec(memory_space=pltpu.HBM)
    in_vmem = pl.BlockSpec(memory_space=pltpu.VMEM)
    dma = pltpu.SemaphoreType.DMA
    modes, factor = pl.pallas_call(
        functools.partial(kernel, point_total),
        out_shape=(
            jax.ShapeDtypeStruct((NB, per, rows, LANES), f32),
            jax.ShapeDtypeStruct((per, 2, NB, NB), f32),
        ),
        in_specs=[in_hbm] * 4,
        out_specs=(in_vmem, in_vmem),
        scratch_shapes=[
            pltpu.VMEM((points, NFFT, 2, LANES), f32),
            pltpu.VMEM((4 * KF, 2 * NFFT), jnp.bfloat16),
            pltpu.VMEM((2, KF, LANES), f32),
            pltpu.VMEM((points, LANES), f32),
            pltpu.VMEM((rows, LANES), f32),
            pltpu.VMEM((NB, per, rows, LANES), f32),
            pltpu.VMEM((rows, LANES), f32),
            pltpu.VMEM((NB, 8, LANES), f32),
            pltpu.VMEM((8, LANES), f32),
            pltpu.VMEM((NB, 8, LANES), f32),
            pltpu.VMEM((per, NB, rows, LANES), f32),
            pltpu.VMEM((per, NB, rows, LANES), f32),
            pltpu.VMEM((NB, rows, LANES), f32),
            pltpu.VMEM((SLOTS * 8, LANES), f32),
            pltpu.VMEM((SLOTS, 8, LANES), f32),
            pltpu.VMEM((8, LANES), f32),
            pltpu.VMEM((1, LANES), f32),
            pltpu.VMEM((8, LANES), f32),
            pltpu.VMEM((1, LANES), f32),
            pltpu.VMEM((8, LANES), f32),
            pltpu.VMEM((1, LANES), f32),
            pltpu.VMEM((others, 8, LANES), f32),
            pltpu.VMEM((others, 1, LANES), f32),
            dma((points // 4,)),
            dma((3,)),
            dma,
            dma((per,)),
            dma,
            dma,
            dma((2,)),
            dma((2, 2)),
            dma((2, 2)),
        ],
        compiler_params=pltpu.CompilerParams(
            collective_id=0, has_side_effects=True, vmem_limit_bytes=48 * 2**20
        ),
    )(*(pltpu.with_memory_space_constraint(v, pltpu.HBM) for v in operands))
    modes, factor = pl.pallas_call(
        writer,
        out_shape=(jax.ShapeDtypeStruct(modes.shape, f32), jax.ShapeDtypeStruct(factor.shape, f32)),
        in_specs=[in_vmem] * 2,
        out_specs=(in_hbm, in_hbm),
        scratch_shapes=[dma((NB + 1,))],
        compiler_params=pltpu.CompilerParams(vmem_limit_bytes=8 * 2**20),
    )(modes, factor)
    modes = modes.reshape(NB, per, points, 2, LANES).transpose(0, 1, 3, 2, 4)
    return (modes.reshape(NB, per, 2, cell_count), factor)


def solution(mesh):
    placed = (P("tm", None, "space"), P("space"))
    return jax.shard_map(
        body,
        mesh=mesh,
        in_specs=placed,
        out_specs=(P(None, "tm", None, "space"), P("tm", None, None, None)),
        check_vma=False,
    )
```

```python
import functools
import math

import jax
import jax.numpy as jnp
import ml_dtypes
import numpy as np
from jax import lax
from jax.experimental import pallas as pl
from jax.experimental.pallas import tpu as pltpu
from jax.sharding import PartitionSpec as P

NB = 8
NFFT = 256
KF = 64
LANES = 128
EARLY = 3
SPLIT = 6
FILL = 4
WINDOW = 8
MESH = pl.DeviceIdType.MESH

PAIRS_RE = [(a, b) for a in range(NB) for b in range(a, NB)]
PAIRS_IM = [(a, b) for a in range(NB) for b in range(a + 1, NB)]
SLOT_RE = {pair: i for i, pair in enumerate(PAIRS_RE)}
SLOT_IM = {pair: len(PAIRS_RE) + i for i, pair in enumerate(PAIRS_IM)}
SLOTS = len(PAIRS_RE) + len(PAIRS_IM)


def tables():
    j = np.arange(NFFT)
    k = np.arange(KF)
    window = 0.54 - 0.46 * np.cos(2.0 * math.pi * j / NFFT)
    angles = 2.0 * math.pi * (k[:, None] * j[None, :] % NFFT) / NFFT
    cos_tab = window * np.cos(angles)
    sin_tab = window * np.sin(angles)
    full = np.zeros((2, KF, NFFT, 2))
    full[0, :, :, 0] = cos_tab
    full[0, :, :, 1] = sin_tab
    full[1, :, :, 0] = -sin_tab
    full[1, :, :, 1] = cos_tab
    full = full.reshape(2 * KF, 2 * NFFT).astype(np.float32)
    high = full.astype(ml_dtypes.bfloat16)
    low = (full - high.astype(np.float32)).astype(ml_dtypes.bfloat16)
    ones = np.ones((1, LANES))
    window_re = (cos_tab.sum(1)[:, None] * ones).astype(np.float32)
    window_im = (-sin_tab.sum(1)[:, None] * ones).astype(np.float32)
    return np.concatenate([high, low], 0), np.stack([window_re, window_im], 0)


def turned(z, even):
    return jnp.where(even, pltpu.roll(z, 7, 0), -pltpu.roll(z, 1, 0))


def cholesky(gram_re, gram_im):
    up_re, up_im, diag_inv = {}, {}, {}
    for j in range(NB):
        pivot = gram_re[j, j]
        for k in range(j):
            pivot = pivot - (up_re[k, j] * up_re[k, j] + up_im[k, j] * up_im[k, j])
        inv = lax.rsqrt(pivot)
        inv = inv * (1.5 - 0.5 * ((pivot * inv) * inv))
        diag_inv[j] = inv
        up_re[j, j] = pivot * inv
        for i in range(j + 1, NB):
            acc_re, acc_im = gram_re[j, i], gram_im[j, i]
            for k in range(j):
                acc_re = acc_re - (up_re[k, j] * up_re[k, i] + up_im[k, j] * up_im[k, i])
                acc_im = acc_im - (up_re[k, j] * up_im[k, i] - up_im[k, j] * up_re[k, i])
            up_re[j, i] = acc_re * inv
            up_im[j, i] = acc_im * inv
    inv_re, inv_im = {}, {}
    for j in range(NB):
        inv_re[j, j] = diag_inv[j]
        for i in range(j - 1, -1, -1):
            acc_re = up_re[i, j] * inv_re[j, j]
            acc_im = up_im[i, j] * inv_re[j, j]
            for k in range(i + 1, j):
                acc_re = acc_re + up_re[i, k] * inv_re[k, j] - up_im[i, k] * inv_im[k, j]
                acc_im = acc_im + up_re[i, k] * inv_im[k, j] + up_im[i, k] * inv_re[k, j]
            inv_re[i, j] = -acc_re * diag_inv[i]
            inv_im[i, j] = -acc_im * diag_inv[i]
    return up_re, up_im, inv_re, inv_im


def kernel(
    point_total, x_hbm, w_hbm, tab_hbm, win_hbm, modes, factor_ref,
    xs, tab, win, wgt, wgt2, spec, sums, sums_in, mean_part, mean, recv, turn, prod, acc, inverse,
    share_0, share_1, core_in_0, core_in_1, half_0, half_1, space_in_0, space_in_1,
    x_sem, in_sem, send_sem, recv_sem, sums_sem, mean_sem, small_sem, core_sem, space_sem,
):
    share, core_in = (share_0, share_1), (core_in_0, core_in_1)
    half, space_in = (half_0, half_1), (space_in_0, space_in_1)
    tm = lax.axis_index("tm")
    sp = lax.axis_index("space")
    points = xs.shape[0]
    rows = 2 * points
    steps = points // 4
    per = KF // NB

    z_hi, y, core = lax.div(sp, 8), lax.rem(lax.div(sp, 2), 4), lax.rem(sp, 2)
    near_first = [(0, 1), (1, 0), (3, 0), (1, 1), (3, 1), (2, 0), (2, 1)]
    mates = [lax.rem(lax.div(tm, 2) + dx, 4) * 2 + lax.rem(tm + dz, 2) for dx, dz in near_first]
    core_peer = z_hi * 8 + y * 2 + (1 - core)
    around = [(dz, dy) for dz in range(4) for dy in range(4) if (dz, dy) != (0, 0)]
    around.sort(key=lambda way: -2 * min(way[0], 4 - way[0]) - min(way[1], 4 - way[1]))
    space_peers = [
        lax.rem(z_hi + dz, 4) * 8 + lax.rem(y + dy, 4) * 2 + core for dz, dy in around
    ]

    def x_copy(pt):
        return pltpu.make_async_copy(x_hbm.at[:, pt], xs.at[pt], x_sem.at[pt // 4])

    barrier = pltpu.get_barrier_semaphore()
    for peer in [*space_peers, core_peer]:
        pl.semaphore_signal(barrier, 1, device_id=(tm, peer), device_id_type=MESH)
    for mate in mates:
        pl.semaphore_signal(barrier, 1, device_id=(mate, sp), device_id_type=MESH)

    tab_copy = pltpu.make_async_copy(tab_hbm, tab, in_sem.at[0])
    win_copy = pltpu.make_async_copy(win_hbm, win, in_sem.at[1])
    wgt_copy = pltpu.make_async_copy(w_hbm, wgt, in_sem.at[2])
    for pt in range(4):
        x_copy(pt).start()
    tab_copy.start()
    win_copy.start()
    for pt in range(4, points):
        x_copy(pt).start()
    wgt_copy.start()

    row8 = lax.broadcasted_iota(jnp.int32, (8, LANES), 0)
    lane8 = lax.broadcasted_iota(jnp.int32, (8, LANES), 1)
    even = lax.rem(row8, 2) == 0
    spec_rows = spec.reshape(KF * rows, LANES)

    def remote(src, dst, recv_at, mate=None, peer=None, sent=None):
        return pltpu.make_async_remote_copy(
            src, dst, send_sem if sent is None else sent, recv_at,
            device_id=(tm if mate is None else mate, sp if peer is None else peer), device_id_type=MESH,
        )

    def transform_step(q):
        pltpu.make_async_copy(xs.at[pl.ds(4 * q, 4)], xs.at[pl.ds(4 * q, 4)], x_sem.at[q]).wait()
        highs, lows, bases = [], [], []
        totals = None
        for i in range(4):
            v = xs.at[4 * q + i].reshape(2 * NFFT, LANES)[...]
            base = v[0:8]
            base = base + pltpu.roll(base, 4, 0)
            base = (base + pltpu.roll(base, 2, 0)) * 0.25
            d = v.reshape(NFFT // 4, 8, LANES) - base[None]
            total = jnp.sum(d, axis=0)
            total = total + pltpu.roll(total, 4, 0)
            total = total + pltpu.roll(total, 2, 0) + base * NFFT
            totals = total if i == 0 else jnp.where(lax.div(row8, 2) == i, total, totals)
            d = d.reshape(2 * NFFT, LANES)
            high = d.astype(jnp.bfloat16)
            highs.append(high)
            lows.append((d - high.astype(jnp.float32)).astype(jnp.bfloat16))
            bases.append(base)
        both = jnp.dot(tab[...], jnp.concatenate(highs, 1), preferred_element_type=jnp.float32)
        rest = jnp.dot(tab[: 2 * KF], jnp.concatenate(lows, 1), preferred_element_type=jnp.float32)
        out = both[: 2 * KF] + both[2 * KF :] + rest
        for i in range(4):
            at = slice(i * LANES, (i + 1) * LANES)
            base_re, base_im = bases[i][0:1], bases[i][1:2]
            spec_rows[pl.ds(8 * q + 2 * i, KF, stride=rows), :] = (
                out[:KF, at] + (win[0] * base_re - win[1] * base_im)
            )
            spec_rows[pl.ds(8 * q + 2 * i + 1, KF, stride=rows), :] = (
                out[KF:, at] + (win[0] * base_im + win[1] * base_re)
            )
        sums[pl.ds(pl.multiple_of(8 * q, 8), 8), :] = totals

    def early_sends(q):
        at = pl.ds(pl.multiple_of(8 * q, 8), 8)
        for mate in mates:
            remote(
                spec.at[mate, pl.ds(0, EARLY), at], recv.at[pl.ds(0, EARLY), tm, at], recv_sem.at[0], mate=mate
            ).start()

    def sums_send(q):
        part = sums.at[pl.ds(pl.multiple_of(8 * q, 8), 8)]

        @pl.when(tm != q)
        def _():
            remote(part, sums_in.at[tm], sums_sem, mate=q, sent=small_sem.at[0]).start()

        @pl.when(tm == q)
        def _():
            pltpu.make_async_copy(part, sums_in.at[tm], sums_sem).start()

    tab_copy.wait()
    win_copy.wait()
    transform_step(0)
    pl.semaphore_wait(barrier, len(mates) + 1 + len(space_peers))
    sums_send(0)
    early_sends(0)

    @pl.loop(1, steps)
    def _(q):
        transform_step(q)
        sums_send(q)
        early_sends(q)

    pltpu.make_async_copy(spec.at[tm, pl.ds(0, EARLY)], recv.at[pl.ds(0, EARLY), tm], recv_sem.at[0]).start()
    def sends(f):
        for mate in mates:
            remote(spec.at[mate, f], recv.at[f, tm], recv_sem.at[f], mate=mate).start()
        pltpu.make_async_copy(spec.at[tm, f], recv.at[f, tm], recv_sem.at[f]).start()

    for f in range(EARLY, FILL):
        sends(f)

    pltpu.make_async_copy(sums_in, sums_in, sums_sem).wait()
    part = sums_in[0]
    for a in range(1, NB):
        part = part + sums_in[a]
    mean_part[...] = part * (1.0 / (NB * NFFT))
    for mate in mates:
        remote(mean_part, mean.at[tm], mean_sem, mate=mate, sent=small_sem.at[1]).start()
    pltpu.make_async_copy(mean_part, mean.at[tm], mean_sem).start()
    for f in range(FILL, WINDOW):
        sends(f)
    wgt_copy.wait()
    scaled = wgt[...] / point_total
    wgt2[pl.ds(0, points, stride=2), :] = scaled
    wgt2[pl.ds(1, points, stride=2), :] = scaled
    pltpu.make_async_copy(mean, mean, mean_sem).wait()

    groups = rows // 8

    def gram_step(f, total):
        win_re = jnp.broadcast_to(win[0, pl.ds(per * tm + f, 1), :], (8, LANES))
        win_im = jnp.broadcast_to(win[1, pl.ds(per * tm + f, 1), :], (8, LANES))
        for g in range(groups):
            at = pl.ds(8 * g, 8)
            m = mean[g]
            shift = win_re * m - win_im * turned(m, even)
            weight = wgt2[at, :]
            for a in range(NB):
                z = recv[f, a, at, :] - shift
                recv[f, a, at, :] = z
                turn[f, a, at, :] = turned(z, even)
                prod[a, at, :] = z * weight
        for a in range(NB):
            sums_re = {}
            sums_im = {}
            for g in range(groups):
                at = pl.ds(8 * g, 8)
                p = prod[a, at, :]
                for b in range(a, NB):
                    term = p * recv[f, b, at, :]
                    sums_re[b] = term if g == 0 else sums_re[b] + term
                    if b > a:
                        term = p * turn[f, b, at, :]
                        sums_im[b] = term if g == 0 else sums_im[b] + term
            for b in range(a, NB):
                acc[pl.ds(8 * SLOT_RE[a, b], 8), :] = sums_re[b]
                if b > a:
                    acc[pl.ds(8 * SLOT_IM[a, b], 8), :] = sums_im[b]
        folded = acc[pl.ds(0, SLOTS, stride=8), :]
        for s in range(1, 8):
            folded = folded + acc[pl.ds(s, SLOTS, stride=8), :]
        folded = jnp.concatenate([folded, jnp.zeros((LANES - SLOTS, LANES), jnp.float32)], 0)
        line = lax.dot_general(
            jnp.ones((8, LANES), jnp.float32), folded, (((1,), (1,)), ((), ())),
            precision=lax.Precision.HIGHEST, preferred_element_type=jnp.float32,
        )
        return jnp.where(row8 == f, line, total)

    def core_start(n, total):
        share[n][...] = total
        remote(share[n], core_in[n], core_sem.at[n, 0], peer=core_peer, sent=core_sem.at[n, 1]).start()

    def space_start(n):
        pltpu.make_async_copy(core_in[n], core_in[n], core_sem.at[n, 0]).wait()
        half[n][...] = share[n][...] + core_in[n][...]
        for i, peer in enumerate(space_peers):
            remote(half[n], space_in[n].at[i], space_sem.at[n, 0], peer=peer, sent=space_sem.at[n, 1]).start()

    def factored(n):
        pltpu.make_async_copy(space_in[n], space_in[n], space_sem.at[n, 0]).wait()
        terms = [half[n][...]] + [space_in[n][i] for i in range(len(space_peers))]
        while len(terms) > 1:
            terms = [a + b for a, b in zip(terms[::2], terms[1::2])]
        gram = terms[0]
        if n == 1:
            gram = jnp.broadcast_to(gram, (8, LANES))
            gram = jnp.where(row8 == per - 1, pltpu.roll(gram, SLOTS, 1), gram)
        spread = [jnp.broadcast_to(gram[:, i : i + 1], (8, LANES)) for i in range(SLOTS)]
        gram_re = {pair: spread[SLOT_RE[pair]] for pair in PAIRS_RE}
        gram_im = {pair: spread[SLOT_IM[pair]] for pair in PAIRS_IM}
        zero = jnp.zeros((8, LANES), jnp.float32)
        up_re, up_im, inv_re, inv_im = cholesky(
            gram_re, {**gram_im, **{(j, j): zero for j in range(NB)}}
        )
        for pair in PAIRS_RE:
            inverse[SLOT_RE[pair]] = inv_re[pair]
        for pair in PAIRS_IM:
            inverse[SLOT_IM[pair]] = inv_im[pair]
        lines = zero
        for a, b in PAIRS_RE:
            lines = jnp.where(lane8 == (NB - 1 - a) * NB + b, up_re[a, b], lines)
        for a, b in PAIRS_IM:
            lines = jnp.where(lane8 == NB * NB + (NB - 1 - a) * NB + b, up_im[a, b], lines)
        return lines

    def apply_step(f):
        co_re = {p: jnp.broadcast_to(inverse[SLOT_RE[p], pl.ds(f, 1), :], (8, LANES)) for p in PAIRS_RE}
        co_im = {p: jnp.broadcast_to(inverse[SLOT_IM[p], pl.ds(f, 1), :], (8, LANES)) for p in PAIRS_IM}
        for b in range(NB):
            for g in range(groups):
                at = pl.ds(8 * g, 8)
                total = recv[f, 0, at, :] * co_re[0, b]
                for a in range(1, b + 1):
                    total = total + recv[f, a, at, :] * co_re[a, b]
                for a in range(b):
                    total = total - turn[f, a, at, :] * co_im[a, b]
                modes[b, f, at, :] = total

    pltpu.make_async_copy(recv.at[pl.ds(0, EARLY)], recv.at[pl.ds(0, EARLY)], recv_sem.at[0]).wait()
    def spectrum_step(f, total):
        @pl.when(f >= EARLY)
        def _():
            pltpu.make_async_copy(recv.at[f], recv.at[f], recv_sem.at[f]).wait()

        @pl.when(f + WINDOW < per)
        def _():
            sends(f + WINDOW)

        total = gram_step(f, total)

        @pl.when(f == SPLIT - 1)
        def _():
            core_start(0, total)

        @pl.when(f == SPLIT)
        def _():
            space_start(0)

        return total

    total = lax.fori_loop(0, per, spectrum_step, jnp.zeros((8, LANES), jnp.float32))
    core_start(1, total[SPLIT : SPLIT + 1] + pltpu.roll(total, SLOTS, 1)[per - 1 :])
    space_start(1)
    factor = factored(0)
    pl.loop(0, SPLIT)(apply_step)
    factor = jnp.where(row8 < SPLIT, factor, factored(1))
    pl.loop(SPLIT, per)(apply_step)
    for f in range(per):
        line = jnp.broadcast_to(factor[f : f + 1], (8, LANES))
        for c in range(2):
            upper_half = line if c == 1 else pltpu.roll(line, LANES // 2, 1)
            factor_ref[f, c] = pltpu.roll(upper_half, NB, 1, stride=NB, stride_axis=0)[:, :NB]

    sent = spec.at[pl.ds(0, NB - 1)]
    pltpu.make_async_copy(sent, sent, send_sem).wait()
    sent = sums_in.at[pl.ds(0, NB - 1)]
    for i in range(2):
        pltpu.make_async_copy(sent, sent, small_sem.at[i]).wait()
        pltpu.make_async_copy(core_in[i], core_in[i], core_sem.at[i, 1]).wait()
        pltpu.make_async_copy(space_in[i], space_in[i], space_sem.at[i, 1]).wait()


def writer(modes, factor, modes_out, factor_out, sem):
    copies = [pltpu.make_async_copy(modes.at[b], modes_out.at[b], sem.at[b]) for b in range(NB)]
    copies.append(pltpu.make_async_copy(factor, factor_out, sem.at[NB]))
    for copy in copies:
        copy.start()
    for copy in copies:
        copy.wait()


def body(snapshots, quad_weights):
    cell_count = snapshots.shape[2]
    points = cell_count // LANES
    rows = 2 * points
    per = KF // NB
    point_total = cell_count * lax.axis_size("space")
    others = lax.axis_size("space") // 2 - 1
    x = snapshots.reshape(NFFT, 2, points, LANES).transpose(0, 2, 1, 3)
    tab, win = tables()
    operands = (x, quad_weights.reshape(points, LANES), jnp.asarray(tab), jnp.asarray(win))
    f32 = jnp.float32
    in_hbm = pl.BlockSpec(memory_space=pltpu.HBM)
    in_vmem = pl.BlockSpec(memory_space=pltpu.VMEM)
    dma = pltpu.SemaphoreType.DMA
    modes, factor = pl.pallas_call(
        functools.partial(kernel, point_total),
        out_shape=(
            jax.ShapeDtypeStruct((NB, per, rows, LANES), f32),
            jax.ShapeDtypeStruct((per, 2, NB, NB), f32),
        ),
        in_specs=[in_hbm] * 4,
        out_specs=(in_vmem, in_vmem),
        scratch_shapes=[
            pltpu.VMEM((points, NFFT, 2, LANES), f32),
            pltpu.VMEM((4 * KF, 2 * NFFT), jnp.bfloat16),
            pltpu.VMEM((2, KF, LANES), f32),
            pltpu.VMEM((points, LANES), f32),
            pltpu.VMEM((rows, LANES), f32),
            pltpu.VMEM((NB, per, rows, LANES), f32),
            pltpu.VMEM((rows, LANES), f32),
            pltpu.VMEM((NB, 8, LANES), f32),
            pltpu.VMEM((8, LANES), f32),
            pltpu.VMEM((NB, 8, LANES), f32),
            pltpu.VMEM((per, NB, rows, LANES), f32),
            pltpu.VMEM((per, NB, rows, LANES), f32),
            pltpu.VMEM((NB, rows, LANES), f32),
            pltpu.VMEM((SLOTS * 8, LANES), f32),
            pltpu.VMEM((SLOTS, 8, LANES), f32),
            pltpu.VMEM((8, LANES), f32),
            pltpu.VMEM((1, LANES), f32),
            pltpu.VMEM((8, LANES), f32),
            pltpu.VMEM((1, LANES), f32),
            pltpu.VMEM((8, LANES), f32),
            pltpu.VMEM((1, LANES), f32),
            pltpu.VMEM((others, 8, LANES), f32),
            pltpu.VMEM((others, 1, LANES), f32),
            dma((points // 4,)),
            dma((3,)),
            dma,
            dma((per,)),
            dma,
            dma,
            dma((2,)),
            dma((2, 2)),
            dma((2, 2)),
        ],
        compiler_params=pltpu.CompilerParams(
            collective_id=0, has_side_effects=True, vmem_limit_bytes=48 * 2**20
        ),
    )(*(pltpu.with_memory_space_constraint(v, pltpu.HBM) for v in operands))
    modes, factor = pl.pallas_call(
        writer,
        out_shape=(jax.ShapeDtypeStruct(modes.shape, f32), jax.ShapeDtypeStruct(factor.shape, f32)),
        in_specs=[in_vmem] * 2,
        out_specs=(in_hbm, in_hbm),
        scratch_shapes=[dma((NB + 1,))],
        compiler_params=pltpu.CompilerParams(vmem_limit_bytes=8 * 2**20),
    )(modes, factor)
    modes = modes.reshape(NB, per, points, 2, LANES).transpose(0, 1, 3, 2, 4)
    return (modes.reshape(NB, per, 2, cell_count), factor)


def solution(mesh):
    placed = (P("tm", None, "space"), P("space"))
    return jax.shard_map(
        body,
        mesh=mesh,
        in_specs=placed,
        out_specs=(P(None, "tm", None, "space"), P("tm", None, None, None)),
        check_vma=False,
    )
```
